32 devices in a mesh: dp: 16 (over z, x, core), seq: 2 (over y).
Axes of the slice: x: 2, y: 2, z: 4, core: 2. Of those that a mesh axis runs over, the one named last changes fastest.
Arguments:
- inputs: bfloat16 [16, 256, 1536], P('dp', 'seq'), may hold values from -45 to 45
- dilated_tap_weight: bfloat16 [3, 768, 1536], P(None, 'seq'), may hold values from -0.09375 to 0.09375
- point_weight: bfloat16 [768, 1536], P('seq'), may hold values from -0.21875 to 0.21875
- query_weight: bfloat16 [1536, 1536], P('seq'), may hold values from -0.21875 to 0.21875
- key_weight: bfloat16 [1536, 1536], P('seq'), may hold values from -0.21875 to 0.21875
- value_weight: bfloat16 [1536, 1536], P('seq'), may hold values from -0.15625 to 0.15625
- out_weight: bfloat16 [1536, 1536], P('seq'), may hold values from -0.4375 to 0.4375
- cotangent: bfloat16 [16, 256, 1536], P('dp', 'seq'), may hold values from -6 to 6
Outputs:
- output: bfloat16 [16, 256, 1536], P('dp', 'seq')
- dilated_tap_gradient: float32 [3, 1536, 768], P(None, 'dp', 'seq')
- point_grad: float32 [768, 1536], P('seq', 'dp')
- query_grad: float32 [1536, 1536], P('dp', 'seq')
- key_grad: float32 [1536, 1536], P('dp', 'seq')
- value_grad: float32 [1536, 1536], P('dp', 'seq')
- out_grad: float32 [1536, 1536], P('seq', 'dp')
The draws below stay inside these ranges and needn't reach their ends.
All inputs are finite; a program needn't handle non-finite values.
Results may differ from the reference program's by a relative error of at most 0.033.
Values may be sent and summed in bfloat16 or wider, within the bound.
No kernel may reach another device: no remote copies, remote signals or barrier semaphores. Data moves between devices by JAX's collectives and lax.ppermute only.
A program may use at most 128 MiB of HBM per device.

```python
import math
import jax
import jax.numpy as jnp
from jax import lax

CH = 1536
MID = 768
HEADS = 8
HSIZE = 192
DILATION_STEP = 16
LEN = 256
BATCH = 16
N_SEQ = 2


def draw_inputs(key, part):
    key_rows, key_cols, key_vals = jax.random.split(key, 3)
    row_scale = jnp.exp(jax.random.uniform(key_rows, (BATCH, LEN, 1), jnp.float32, -1.2, 1.1))
    col_scale = jnp.exp(jax.random.uniform(key_cols, (1, 1, CH), jnp.float32, -1.2, 1.1))
    value_rows = jnp.clip(jax.random.normal(key_vals, (BATCH, LEN, CH), jnp.float32), -5.0, 5.0)
    return (value_rows * row_scale * col_scale).astype(jnp.bfloat16)


def shard_levels(stream_key, shape, cuts, low, top_value):
    gain, own = 1.0, jax.random.fold_in(stream_key, 6)
    for dim, shards_of in cuts:
        heights = jnp.exp(jax.random.uniform(jax.random.fold_in(own, dim), (shards_of,), jnp.float32, low / len(cuts), top_value / len(cuts)))
        gain = gain * jnp.repeat(heights, shape[dim] // shards_of).reshape([-1 if axis == dim else 1 for axis in range(len(shape))])
    return gain


def normal_values(rng, shape, scale, reach, cuts=(), held_as=jnp.bfloat16):
    drawn = jax.random.normal(rng, shape, jnp.float32) * scale
    if len(cuts) > 0:
        drawn = shard_levels(rng, shape, cuts, -0.22, 0.18) * drawn
    return jnp.clip(drawn, min=-reach, max=reach).astype(held_as)


def setup_inputs(seed: int = 0) -> dict:
    keys = jax.random.split(jax.random.key(seed), 9)
    return {
        "inputs": draw_inputs(jax.random.fold_in(keys[8], 71), 0),
        "dilated_tap_weight": normal_values(keys[1], (3, MID, CH), (3 * CH) ** -0.5, 0.09375, ((1, 2),)),
        "point_weight": normal_values(keys[2], (MID, CH), MID ** -0.5, 0.21875, ((0, 2),)),
        "query_weight": normal_values(keys[3], (HEADS * HSIZE, CH), (CH // 2) ** -0.5, 0.21875, ((0, 2),)),
        "key_weight": normal_values(keys[4], (HEADS * HSIZE, CH), (CH // 2) ** -0.5, 0.21875, ((0, 2),)),
        "value_weight": normal_values(keys[5], (HEADS * HSIZE, CH), CH ** -0.5, 0.15625, ((0, 2),)),
        "out_weight": normal_values(keys[6], (HEADS * HSIZE, CH), (HEADS * HSIZE // 8) ** -0.5, 0.4375, ((0, 2),)),
        "cotangent": normal_values(keys[7], (BATCH, LEN, CH), 1.0, 6.0, ((0, 16), (1, 2))),
    }


EPSILON = 1e-06
SOFT_CAP = 6.0

def rms_scale(value_rows):
    return lax.rsqrt(lax.optimization_barrier(jnp.mean(value_rows * value_rows, axis=-1, keepdims=True)) + EPSILON)

def rows_shifted(value_rows, tap_shift):
    if tap_shift == 0:
        return value_rows
    padded_rows = jnp.pad(value_rows, ((DILATION_STEP, DILATION_STEP), (0, 0)))
    return padded_rows[DILATION_STEP + tap_shift:DILATION_STEP + tap_shift + value_rows.shape[0]]

def gelu_back(pre_act, upstream):
    return jax.vjp(jax.nn.gelu, pre_act)[1](upstream)[0]

def block_sum(pair_list):
    total = None
    for left_side, right_side in pair_list:
        length = left_side.shape[0]
        inner_len = left_side.shape[1] // N_SEQ
        left_blocks = left_side.reshape(length, N_SEQ, inner_len).astype(jnp.float32)
        right_blocks = right_side.reshape(N_SEQ, inner_len, right_side.shape[1]).astype(jnp.float32)
        partial_value = jnp.einsum('lsk,skc->slc', left_blocks, right_blocks)
        total = partial_value if total is None else total + partial_value
    rounded = lax.optimization_barrier(total.astype(jnp.bfloat16))
    return lax.optimization_barrier(jnp.sum(rounded.astype(jnp.float32), axis=0))

def split_heads(matrix):
    head_count = matrix.shape[1] // HSIZE
    return matrix.reshape(matrix.shape[0], head_count, HSIZE).transpose(1, 0, 2)

def join_heads(stacked):
    return stacked.transpose(1, 0, 2).reshape(stacked.shape[1], -1)

def head_pass(packed):
    query_h, key_h, value_h, dout_h = packed
    inv_root = 1.0 / math.sqrt(HSIZE)
    raw_score = jnp.dot(query_h, key_h.T, preferred_element_type=jnp.float32) * inv_root
    capped = SOFT_CAP * jnp.tanh(raw_score / SOFT_CAP)
    unnormed = jnp.exp(capped)
    soft_weights = unnormed / lax.optimization_barrier(jnp.sum(unnormed, axis=-1, keepdims=True))
    soft_low = soft_weights.astype(jnp.bfloat16)
    out_h = jnp.dot(soft_low, value_h, preferred_element_type=jnp.float32).astype(jnp.bfloat16)
    grad_soft = jnp.dot(dout_h, value_h.T, preferred_element_type=jnp.float32)
    grad_capped = soft_weights * (grad_soft - lax.optimization_barrier(jnp.sum(soft_weights * grad_soft, axis=-1, keepdims=True)))
    ratio = capped / SOFT_CAP
    grad_score = (grad_capped * (1.0 - ratio * ratio)).astype(jnp.bfloat16)
    grad_query = (jnp.dot(grad_score, key_h, preferred_element_type=jnp.float32) * inv_root).astype(jnp.bfloat16)
    grad_key = (jnp.dot(grad_score.T, query_h, preferred_element_type=jnp.float32) * inv_root).astype(jnp.bfloat16)
    grad_value = jnp.dot(soft_low.T, dout_h, preferred_element_type=jnp.float32).astype(jnp.bfloat16)
    return (out_h, grad_query, grad_key, grad_value)

def one_sequence(inputs, cotangent, dilated_tap_weight, point_weight, query_weight, key_weight, value_weight, out_weight):
    inv_tokens = 1.0 / math.sqrt(BATCH * LEN)
    input_full = inputs.astype(jnp.float32)
    gelu_output = jax.nn.gelu(input_full * rms_scale(input_full)).astype(jnp.bfloat16)
    convolution_preact = sum((jnp.dot(rows_shifted(gelu_output, (tap_position - 1) * DILATION_STEP), dilated_tap_weight[tap_position].T, preferred_element_type=jnp.float32) for tap_position in range(3)))
    middle = jax.nn.gelu(convolution_preact).astype(jnp.bfloat16)
    residual = (input_full + block_sum([(middle, point_weight)])).astype(jnp.bfloat16)
    residual_f32 = lax.optimization_barrier(residual).astype(jnp.float32)
    scale = rms_scale(residual_f32)
    normed = (residual_f32 * scale).astype(jnp.bfloat16)
    query_mat = jnp.dot(normed, query_weight.T, preferred_element_type=jnp.float32).astype(jnp.bfloat16)
    key_mat = jnp.dot(normed, key_weight.T, preferred_element_type=jnp.float32).astype(jnp.bfloat16)
    value_mat = jnp.dot(normed, value_weight.T, preferred_element_type=jnp.float32).astype(jnp.bfloat16)
    grad_y = (cotangent.astype(jnp.float32) * inv_tokens).astype(jnp.bfloat16)
    grad_heads = jnp.dot(grad_y, out_weight.T, preferred_element_type=jnp.float32).astype(jnp.bfloat16)
    results = lax.map(head_pass, (split_heads(query_mat), split_heads(key_mat), split_heads(value_mat), split_heads(grad_heads)))
    attended, query_delta, key_delta, value_delta = [join_heads(stacked) for stacked in results]
    output = (residual_f32 + block_sum([(attended, out_weight)])).astype(jnp.bfloat16)
    out_grad = jnp.dot(attended.T, grad_y, preferred_element_type=jnp.float32)
    query_grad = jnp.dot(normed.T, query_delta, preferred_element_type=jnp.float32)
    key_grad = jnp.dot(normed.T, key_delta, preferred_element_type=jnp.float32)
    value_grad = jnp.dot(normed.T, value_delta, preferred_element_type=jnp.float32)
    grad_normed = block_sum([(query_delta, query_weight), (key_delta, key_weight), (value_delta, value_weight)])
    grad_resid = (grad_y.astype(jnp.float32) + scale * grad_normed - residual_f32 * scale ** 3 * lax.optimization_barrier(jnp.mean(grad_normed * residual_f32, axis=-1, keepdims=True))).astype(jnp.bfloat16)
    grad_middle = jnp.dot(grad_resid, point_weight.T, preferred_element_type=jnp.float32)
    convolution_gradient = gelu_back(convolution_preact, grad_middle).astype(jnp.bfloat16)
    point_grad = jnp.dot(middle.T, grad_resid, preferred_element_type=jnp.float32)
    dilated_tap_gradient = jnp.stack([jnp.dot(rows_shifted(gelu_output, (tap_position - 1) * DILATION_STEP).T, convolution_gradient, preferred_element_type=jnp.float32) for tap_position in range(3)])
    return (output, dilated_tap_gradient, point_grad, query_grad, key_grad, value_grad, out_grad)

def reference(inputs, dilated_tap_weight, point_weight, query_weight, key_weight, value_weight, out_weight, cotangent):

    def scan_step(totals, sequence_pair):
        result = one_sequence(sequence_pair[0], sequence_pair[1], dilated_tap_weight, point_weight, query_weight, key_weight, value_weight, out_weight)
        new_totals = tuple((old + fresh for old, fresh in zip(totals, result[1:])))
        return (new_totals, result[0])
    zero_grads = (jnp.zeros((3, CH, MID), jnp.float32), jnp.zeros(point_weight.shape, jnp.float32), jnp.zeros((CH, HEADS * HSIZE), jnp.float32), jnp.zeros((CH, HEADS * HSIZE), jnp.float32), jnp.zeros((CH, HEADS * HSIZE), jnp.float32), jnp.zeros(out_weight.shape, jnp.float32))
    grad_sums, outputs = lax.scan(scan_step, zero_grads, (inputs, cotangent))
    return (outputs, grad_sums[0], grad_sums[1], grad_sums[2], grad_sums[3], grad_sums[4], grad_sums[5])
```

```python
import functools
import math

import jax
import jax.numpy as jnp
from jax import lax
from jax.experimental import pallas as pl
from jax.experimental.pallas import tpu as pltpu
from jax.sharding import PartitionSpec as P

HSIZE = 192
DILATION_STEP = 16
EPSILON = 1e-06
SOFT_CAP = 6.0
GELU_C = math.sqrt(2.0 / math.pi)
GELU_A = 0.044715
BF = jnp.bfloat16
F32 = jnp.float32
VMEM_BYTES = 56 * 1024 * 1024


def gelu(x):
    return 0.5 * x * (1.0 + jnp.tanh(GELU_C * (x + GELU_A * (x * x * x))))


def gelu_slope(x):
    t = jnp.tanh(GELU_C * (x + GELU_A * (x * x * x)))
    return 0.5 * (1.0 + t) + 0.5 * x * (1.0 - t * t) * GELU_C * (1.0 + 3.0 * GELU_A * x * x)


def dot_nn(a, b):
    return lax.dot_general(a, b, (((1,), (0,)), ((), ())), preferred_element_type=F32)


def dot_nt(a, b):
    return lax.dot_general(a, b, (((1,), (1,)), ((), ())), preferred_element_type=F32)


def dot_tn(a, b):
    return lax.dot_general(a, b, (((0,), (0,)), ((), ())), preferred_element_type=F32)


def rms_scale(x):
    return lax.rsqrt(jnp.mean(x * x, axis=-1, keepdims=True) + EPSILON)


def row_chunk(rows):
    return 128 if rows % 128 == 0 else rows


def loop_chunks(count, body):
    if count <= 2:
        for i in range(count):
            body(i)
    else:

        def step(i, carry):
            body(i)
            return carry

        lax.fori_loop(0, count, step, 0)


def rows_at(i, size):
    if isinstance(i, int):
        return pl.ds(i * size, size)
    return pl.ds(pl.multiple_of(i * size, size), size)


def emit_rows(starts, wide, outs):
    group = len(outs)
    for p in range(group):
        out = outs[p]
        ring = starts.shape[0] // group
        size = out.shape[0] // ring
        for k in range(ring):
            at = pl.multiple_of(starts[p * ring + k], 16)
            out[k * size : (k + 1) * size, :] = wide[pl.ds(at, size), :]


def shifted_sum(first, middle, last, offset):
    length = middle.shape[0]
    step = DILATION_STEP
    pos = lax.rem(lax.broadcasted_iota(jnp.int32, (length, 1), 0) + offset, length)
    down = jnp.concatenate([first[length - step :], first[: length - step]], axis=0)
    up = jnp.concatenate([last[step:], last[:step]], axis=0)
    return jnp.where(pos >= step, down, 0.0) + middle + jnp.where(pos < length - step, up, 0.0)


def call(kernel, out_shape, operands, smem=1, scratch=(), flops=0):
    specs = [pl.BlockSpec(memory_space=pltpu.SMEM)] * smem
    specs += [pl.BlockSpec(memory_space=pltpu.VMEM)] * (len(operands) - smem)
    moved = sum(math.prod(t.shape) * t.dtype.itemsize for t in list(operands) + list(out_shape))
    return pl.pallas_call(
        kernel,
        out_shape=out_shape,
        in_specs=specs,
        out_specs=[pl.BlockSpec(memory_space=pltpu.VMEM)] * len(out_shape),
        scratch_shapes=list(scratch),
        compiler_params=pltpu.CompilerParams(vmem_limit_bytes=VMEM_BYTES),
        cost_estimate=pl.CostEstimate(flops=flops, bytes_accessed=moved, transcendentals=0),
    )(*operands)


def shape_of(rows, cols, dtype=BF):
    return jax.ShapeDtypeStruct((rows, cols), dtype)


def conv_block(starts, offset, pieces, taps, point, ring_rows, group):
    count = len(pieces)
    rows = pieces[0].shape[0]
    length, channels = rows * count, pieces[0].shape[1]
    inner = point.shape[0]

    def kernel(*refs):
        starts_ref, offset_ref = refs[:2]
        ins = refs[2 : 2 + count]
        taps_ref, point_ref = refs[2 + count : 4 + count]
        pre_ref, mid_ref, part_ref = refs[4 + count : 7 + count]
        sent = refs[7 + count : 7 + count + group]
        act, wide, prod = refs[7 + count + group :]
        size = row_chunk(rows)
        for j in range(count):

            def body(i, j=j):
                x = ins[j][rows_at(i, size), :].astype(F32)
                a = gelu(x * rms_scale(x)).astype(BF)
                if isinstance(i, int):
                    here = pl.ds(j * rows + i * size, size)
                else:
                    here = pl.ds(pl.multiple_of(j * rows + i * size, size), size)
                act[here, :] = a
                wide[:, here] = a.T

            loop_chunks(rows // size, body)
        emit_rows(starts_ref, wide, sent)
        big = min(256, length)

        def product(i):
            here = rows_at(i, big)
            prod[here, :] = dot_nt(act[here, :], taps_ref[...])

        loop_chunks(length // big, product)
        pre = shifted_sum(
            prod[:, :inner], prod[:, inner : 2 * inner], prod[:, 2 * inner :], offset_ref[0]
        )
        pre_ref[...] = pre
        mid_ref[...] = gelu(pre).astype(BF)

        def back(i):
            here = rows_at(i, big)
            part_ref[here, :] = dot_nn(mid_ref[here, :], point_ref[...]).astype(BF)

        loop_chunks(length // big, back)

    outs = [shape_of(length, inner, F32), shape_of(length, inner), shape_of(length, channels)]
    outs += [shape_of(ring_rows, length)] * group
    scratch = [
        pltpu.VMEM((length, channels), BF),
        pltpu.VMEM((channels, length), BF),
        pltpu.VMEM((length, 3 * inner), F32),
    ]
    res = call(
        kernel, outs, [starts, offset, *pieces, taps, point], 2, scratch, 8 * length * inner * channels
    )
    return res[0], res[1], res[2], res[3:]


def norm_block(starts, pieces, part, moved, ring_rows, group):
    count = len(pieces)
    rows = pieces[0].shape[0]
    length, channels = part.shape

    def kernel(*refs):
        starts_ref = refs[0]
        ins = refs[1 : 1 + count]
        part_ref = refs[1 + count]
        adds = refs[2 + count : 2 + count + len(moved)]
        rest = refs[2 + count + len(moved) :]
        res_ref, norm_ref = rest[:2]
        sent = rest[2 : 2 + group]
        wide = rest[2 + group]
        size = row_chunk(rows)
        for j in range(count):

            def body(i, j=j):
                if isinstance(i, int):
                    here = pl.ds(j * rows + i * size, size)
                else:
                    here = pl.ds(pl.multiple_of(j * rows + i * size, size), size)
                total = part_ref[here, :].astype(F32)
                if adds:
                    total = total + adds[j][rows_at(i, size), :].astype(F32)
                res = (ins[j][rows_at(i, size), :].astype(F32) + total).astype(BF)
                res_ref[here, :] = res
                res = res.astype(F32)
                a = (res * rms_scale(res)).astype(BF)
                norm_ref[here, :] = a
                wide[:, here] = a.T

            loop_chunks(rows // size, body)
        emit_rows(starts_ref, wide, sent)

    outs = [shape_of(length, channels), shape_of(length, channels)]
    outs += [shape_of(ring_rows, length)] * group
    scratch = [pltpu.VMEM((channels, length), BF)]
    res = call(kernel, outs, [starts, *pieces, part, *moved], 1, scratch)
    return res[0], res[1], res[2:]


def widen_block(starts, pieces, ring_rows, group):
    count = len(pieces)
    rows, channels = pieces[0].shape
    length = rows * count

    def kernel(*refs):
        starts_ref = refs[0]
        ins = refs[1 : 1 + count]
        whole_ref = refs[1 + count]
        sent = refs[2 + count : 2 + count + group]
        wide = refs[2 + count + group]
        size = row_chunk(rows)
        for j in range(count):

            def body(i, j=j):
                if isinstance(i, int):
                    here = pl.ds(j * rows + i * size, size)
                else:
                    here = pl.ds(pl.multiple_of(j * rows + i * size, size), size)
                a = ins[j][rows_at(i, size), :]
                whole_ref[here, :] = a
                wide[:, here] = a.T

            loop_chunks(rows // size, body)
        emit_rows(starts_ref, wide, sent)

    outs = [shape_of(length, channels)] + [shape_of(ring_rows, length)] * group
    scratch = [pltpu.VMEM((channels, length), BF)]
    res = call(kernel, outs, [starts, *pieces], 1, scratch)
    return res[0], res[1:]


def attention_block(normed, grad_y, query_w, key_w, value_w, out_w):
    length, channels = normed.shape
    features = query_w.shape[0]
    heads = features // HSIZE
    per_step = 2 if heads % 2 == 0 else 1
    width = per_step * HSIZE
    inv_root = 1.0 / math.sqrt(HSIZE)
    chunk = min(256, length)

    def kernel(n_ref, gy_ref, wq, wk, wv, wo, dq_ref, dk_ref, dv_ref, at_ref, dn_ref, acc):
        step = pl.program_id(0)
        n = n_ref[...]
        gy = gy_ref[...]
        dqs, dks, dvs, ats = [], [], [], []
        for h in range(per_step):
            rows = pl.ds(h * HSIZE, HSIZE)
            q = dot_nt(n, wq[rows, :]).astype(BF)
            k = dot_nt(n, wk[rows, :]).astype(BF)
            v = dot_nt(n, wv[rows, :]).astype(BF)
            g = dot_nt(gy, wo[rows, :]).astype(BF)
            dq, at = [], []
            dk = dv = None
            for c in range(length // chunk):
                qc = q[c * chunk : (c + 1) * chunk]
                gc = g[c * chunk : (c + 1) * chunk]
                ratio = jnp.tanh(dot_nt(qc, k) * (inv_root / SOFT_CAP))
                unnormed = jnp.exp(SOFT_CAP * ratio)
                soft = unnormed / jnp.sum(unnormed, axis=-1, keepdims=True)
                low = soft.astype(BF)
                at.append(dot_nn(low, v))
                gs = dot_nt(gc, v)
                gs = soft * (gs - jnp.sum(soft * gs, axis=-1, keepdims=True))
                gs = (gs * (1.0 - ratio * ratio)).astype(BF)
                dq.append(dot_nn(gs, k) * inv_root)
                dk_c = dot_tn(gs, qc)
                dv_c = dot_tn(low, gc)
                dk = dk_c if dk is None else dk + dk_c
                dv = dv_c if dv is None else dv + dv_c
            join = (lambda parts: parts[0] if len(parts) == 1 else jnp.concatenate(parts, axis=0))
            dqs.append(join(dq))
            ats.append(join(at))
            dks.append(dk * inv_root)
            dvs.append(dv)
        side = (lambda parts: parts[0] if len(parts) == 1 else jnp.concatenate(parts, axis=1))
        dq, dk, dv, at = [side(t).astype(BF) for t in (dqs, dks, dvs, ats)]
        dq_ref[...] = dq
        dk_ref[...] = dk
        dv_ref[...] = dv
        at_ref[...] = at
        total = dot_nn(dq, wq[...]) + dot_nn(dk, wk[...]) + dot_nn(dv, wv[...])

        @pl.when(step == 0)
        def _():
            acc[...] = total

        @pl.when(step > 0)
        def _():
            acc[...] += total

        @pl.when(step == pl.num_programs(0) - 1)
        def _():
            dn_ref[...] = acc[...].astype(BF)

    whole = pl.BlockSpec((length, channels), lambda i: (0, 0))
    weight = pl.BlockSpec((width, channels), lambda i: (i, 0))
    column = pl.BlockSpec((length, width), lambda i: (0, i))
    return pl.pallas_call(
        kernel,
        grid=(heads // per_step,),
        out_shape=[shape_of(length, features)] * 4 + [shape_of(length, channels)],
        in_specs=[whole, whole, weight, weight, weight, weight],
        out_specs=[column] * 4 + [whole],
        scratch_shapes=[pltpu.VMEM((length, channels), F32)],
        compiler_params=pltpu.CompilerParams(vmem_limit_bytes=VMEM_BYTES),
        cost_estimate=pl.CostEstimate(
            flops=14 * length * features * channels + 12 * length * length * features,
            bytes_accessed=2 * (4 * features * channels + 3 * length * channels),
            transcendentals=2 * heads * length * length,
        ),
    )(normed, grad_y, query_w, key_w, value_w, out_w)


def back_block(starts, residual, grad_y, part, moved, pre, point, ring_rows, group):
    length, channels = residual.shape
    inner = point.shape[0]
    rows = length // max(1, len(moved))

    def kernel(*refs):
        starts_ref, res_ref, gy_ref, part_ref = refs[:4]
        adds = refs[4 : 4 + len(moved)]
        pre_ref, point_ref = refs[4 + len(moved) : 6 + len(moved)]
        rest = refs[6 + len(moved) :]
        gc_ref = rest[0]
        sent = rest[1 : 1 + group]
        wide, resid_grad = rest[1 + group :]
        size = row_chunk(rows)
        for j in range(length // rows):

            def body(i, j=j):
                if isinstance(i, int):
                    here = pl.ds(j * rows + i * size, size)
                else:
                    here = pl.ds(pl.multiple_of(j * rows + i * size, size), size)
                gn = part_ref[here, :].astype(F32)
                if adds:
                    gn = gn + adds[j][rows_at(i, size), :].astype(F32)
                res = res_ref[here, :].astype(F32)
                scale = rms_scale(res)
                inner_mean = jnp.mean(gn * res, axis=-1, keepdims=True)
                a = gy_ref[here, :].astype(F32) + (
                    scale * gn - res * (scale * scale * scale) * inner_mean
                )
                a = a.astype(BF)
                resid_grad[here, :] = a
                wide[:, here] = a.T

            loop_chunks(rows // size, body)
        big = min(256, length)

        def product(i):
            here = rows_at(i, big)
            gm = dot_nt(resid_grad[here, :], point_ref[...])
            gc_ref[here, :] = (gelu_slope(pre_ref[here, :]) * gm).astype(BF)

        loop_chunks(length // big, product)
        emit_rows(starts_ref, wide, sent)

    outs = [shape_of(length, inner)] + [shape_of(ring_rows, length)] * group
    scratch = [pltpu.VMEM((channels, length), BF), pltpu.VMEM((length, channels), BF)]
    res = call(
        kernel,
        outs,
        [starts, residual, grad_y, part, *moved, pre, point],
        1,
        scratch,
        2 * length * inner * channels,
    )
    return res[0], res[1:]


def weight_sum(wides, narrows):
    group = len(wides)
    rows, length = wides[0].shape
    cols = narrows[0].shape[1]

    def kernel(*refs):
        total = None
        for a, b in zip(refs[:group], refs[group : 2 * group]):
            term = dot_nn(a[...], b[...])
            total = term if total is None else total + term
        refs[-1][...] = total.astype(BF)

    return call(
        kernel,
        [shape_of(rows, cols)],
        [*wides, *narrows],
        0,
        (),
        2 * group * rows * length * cols,
    )[0]


def tap_sum(offset, wides, narrows):
    group = len(wides)
    rows, length = wides[0].shape
    inner = narrows[0].shape[1]
    step = DILATION_STEP

    def kernel(offset_ref, *refs):
        pos = lax.rem(
            lax.broadcasted_iota(jnp.int32, (length, 1), 0) + offset_ref[0], length
        )
        total = [None, None, None]
        for a_ref, b_ref in zip(refs[:group], refs[group : 2 * group]):
            a = a_ref[...]
            b = b_ref[...]
            up = jnp.concatenate([b[step:], b[:step]], axis=0).astype(F32)
            down = jnp.concatenate([b[length - step :], b[: length - step]], axis=0).astype(F32)
            first = jnp.where(pos < length - step, up, 0.0).astype(BF)
            last = jnp.where(pos >= step, down, 0.0).astype(BF)
            for k, moved in enumerate((first, b, last)):
                term = dot_nn(a, moved)
                total[k] = term if total[k] is None else total[k] + term
        for k in range(3):
            refs[-1][:, k * inner : (k + 1) * inner] = total[k].astype(BF)

    return call(
        kernel,
        [shape_of(rows, 3 * inner)],
        [offset, *wides, *narrows],
        1,
        (),
        6 * group * rows * length * inner,
    )[0]


def shards(
    inputs,
    dilated_tap_weight,
    point_weight,
    query_weight,
    key_weight,
    value_weight,
    out_weight,
    cotangent,
):
    channels = inputs.shape[2]
    own = inputs[0]
    rows = own.shape[0]
    n_seq = lax.axis_size("seq")
    n_dp = lax.axis_size("dp")
    length = rows * n_seq
    pair = n_seq == 2
    group = 4 if n_dp % 4 == 0 else 2 if n_dp % 2 == 0 else 1
    ring = n_dp // group
    block = channels // n_dp
    ring_rows = ring * block
    inner = point_weight.shape[0]
    features = query_weight.shape[0]
    inv_tokens = 1.0 / math.sqrt(inputs.shape[0] * n_dp * length)

    me_dp = lax.axis_index("dp")
    me_seq = lax.axis_index("seq")
    me_ring, me_group = me_dp // group, me_dp % group
    order = jnp.arange(group, dtype=jnp.int32)[:, None]
    turn = jnp.arange(ring, dtype=jnp.int32)[None, :]
    starts = (((me_ring + turn) % ring * group + (me_group ^ order)) * block).reshape(-1)
    starts = starts.astype(jnp.int32)
    offset = (me_seq * rows if pair else jnp.int32(0)).astype(jnp.int32).reshape(1)

    def swap_seq(x):
        return lax.ppermute(x, "seq", [(0, 1), (1, 0)])

    def to_peer(x, bits):
        if bits == 0:
            return x
        return lax.ppermute(x, "dp", [(i, i ^ bits) for i in range(n_dp)])

    def gather_seq(x):
        if pair:
            return [x, swap_seq(x)]
        return [lax.all_gather(x, "seq", axis=0, tiled=True)]

    def add_seq(part):
        if pair:
            return part, [swap_seq(part[rows:]), swap_seq(part[:rows])]
        summed = lax.psum_scatter(part, "seq", scatter_dimension=0, tiled=True)
        return lax.all_gather(summed, "seq", axis=0, tiled=True), []

    def share_wide(pieces):
        return [to_peer(piece, p) for p, piece in enumerate(pieces)]

    def share_narrow(x):
        got = [x]
        if group >= 2:
            got.append(to_peer(x, 1))
        if group >= 4:
            far = to_peer(x, 2)
            got += [far, to_peer(far, 1)]
        return got

    def reduce_ring(total):
        out = total[:block].astype(F32)
        for k in range(1, ring):
            hops = [(i, ((i // group + k) % ring) * group + i % group) for i in range(n_dp)]
            moved = lax.ppermute(total[k * block : (k + 1) * block], "dp", hops)
            out = out + moved.astype(F32)
        return out

    pieces = gather_seq(own)
    grad_own = (cotangent[0].astype(F32) * inv_tokens).astype(BF)
    taps = dilated_tap_weight.reshape(3 * inner, channels)
    pre, middle, part, act_sent = conv_block(
        starts, offset, pieces, taps, point_weight, ring_rows, group
    )
    grad_pieces = gather_seq(grad_own)
    part, moved = add_seq(part)
    grad_y, grad_sent = widen_block(starts, grad_pieces, ring_rows, group)
    residual, normed, norm_sent = norm_block(starts, pieces, part, moved, ring_rows, group)
    act_wide = share_wide(act_sent)
    middle_all = share_narrow(middle)
    grad_wide = share_wide(grad_sent)
    norm_wide = share_wide(norm_sent)

    dq, dk, dv, attended, grad_part = attention_block(
        normed, grad_y, query_weight, key_weight, value_weight, out_weight
    )
    grad_part, grad_moved = add_seq(grad_part)

    attn_part = dot_nn(attended, out_weight).astype(BF)
    if pair:
        attn_rows = attn_part[:rows].astype(F32) + swap_seq(attn_part[rows:]).astype(F32)
    else:
        attn_rows = lax.psum_scatter(attn_part, "seq", scatter_dimension=0, tiled=True)
        attn_rows = attn_rows.astype(F32)
    if pair:
        res_own = residual[:rows]
    else:
        res_own = lax.dynamic_slice_in_dim(residual, me_seq * rows, rows, 0)
    output = (res_own.astype(F32) + attn_rows).astype(BF)[None]

    query_sum = reduce_ring(weight_sum(norm_wide, share_narrow(dq)))
    key_sum = reduce_ring(weight_sum(norm_wide, share_narrow(dk)))
    value_sum = reduce_ring(weight_sum(norm_wide, share_narrow(dv)))
    out_sum = reduce_ring(weight_sum(grad_wide, share_narrow(attended))).T

    grad_conv, resid_sent = back_block(
        starts, residual, grad_y, grad_part, grad_moved, pre, point_weight, ring_rows, group
    )
    tap_total = reduce_ring(tap_sum(offset, act_wide, share_narrow(grad_conv)))
    tap_total = tap_total.reshape(block, 3, inner).transpose(1, 0, 2)
    point_sum = reduce_ring(weight_sum(share_wide(resid_sent), middle_all)).T
    return (output, tap_total, point_sum, query_sum, key_sum, value_sum, out_sum)


def solution(mesh):
    placed = (
        P("dp", "seq", None),
        P(None, "seq", None),
        P("seq", None),
        P("seq", None),
        P("seq", None),
        P("seq", None),
        P("seq", None),
        P("dp", "seq", None),
    )
    return jax.shard_map(
        shards,
        mesh=mesh,
        in_specs=placed,
        out_specs=(
            P("dp", "seq", None),
            P(None, "dp", "seq"),
            P("seq", "dp"),
            P("dp", "seq"),
            P("dp", "seq"),
            P("dp", "seq"),
            P("seq", "dp"),
        ),
        check_vma=False,
    )
```

```python
import functools
import math

import jax
import jax.numpy as jnp
from jax import lax
from jax.experimental import pallas as pl
from jax.experimental.pallas import tpu as pltpu
from jax.sharding import PartitionSpec as P

HSIZE = 192
DILATION_STEP = 16
EPSILON = 1e-06
SOFT_CAP = 6.0
GELU_C = math.sqrt(2.0 / math.pi)
GELU_A = 0.044715
BF = jnp.bfloat16
F32 = jnp.float32
VMEM_BYTES = 56 * 1024 * 1024
NO_COST = pl.CostEstimate(flops=0, bytes_accessed=0, transcendentals=0)


def gelu(x):
    return 0.5 * x * (1.0 + jnp.tanh(GELU_C * (x + GELU_A * (x * x * x))))


def gelu_slope(x):
    t = jnp.tanh(GELU_C * (x + GELU_A * (x * x * x)))
    return 0.5 * (1.0 + t) + 0.5 * x * (1.0 - t * t) * GELU_C * (1.0 + 3.0 * GELU_A * x * x)


def dot_nn(a, b):
    return lax.dot_general(a, b, (((1,), (0,)), ((), ())), preferred_element_type=F32)


def dot_nt(a, b):
    return lax.dot_general(a, b, (((1,), (1,)), ((), ())), preferred_element_type=F32)


def dot_tn(a, b):
    return lax.dot_general(a, b, (((0,), (0,)), ((), ())), preferred_element_type=F32)


def rms_scale(x):
    return lax.rsqrt(jnp.mean(x * x, axis=-1, keepdims=True) + EPSILON)


def row_chunk(rows):
    return 128 if rows % 128 == 0 else rows


def loop_chunks(count, body):
    if count <= 2:
        for i in range(count):
            body(i)
    else:

        def step(i, carry):
            body(i)
            return carry

        lax.fori_loop(0, count, step, 0)


def rows_at(i, size):
    if isinstance(i, int):
        return pl.ds(i * size, size)
    return pl.ds(pl.multiple_of(i * size, size), size)


def emit_rows(starts, wide, outs, rows):
    parts = starts.shape[0] // len(outs)
    size = rows // parts
    for p, out in enumerate(outs):
        for k in range(parts):
            at = pl.multiple_of(starts[p * parts + k], 16)
            out[k * size : (k + 1) * size, :] = wide[pl.ds(at, size), :]


def shifted_sum(first, middle, last, offset):
    length = middle.shape[0]
    step = DILATION_STEP
    pos = lax.rem(lax.broadcasted_iota(jnp.int32, (length, 1), 0) + offset, length)
    down = jnp.concatenate([first[length - step :], first[: length - step]], axis=0)
    up = jnp.concatenate([last[step:], last[:step]], axis=0)
    return jnp.where(pos >= step, down, 0.0) + middle + jnp.where(pos < length - step, up, 0.0)


def call(kernel, out_shape, operands, smem=1, scratch=()):
    specs = [pl.BlockSpec(memory_space=pltpu.SMEM)] * smem
    specs += [pl.BlockSpec(memory_space=pltpu.VMEM)] * (len(operands) - smem)
    return pl.pallas_call(
        kernel,
        out_shape=out_shape,
        in_specs=specs,
        out_specs=[pl.BlockSpec(memory_space=pltpu.VMEM)] * len(out_shape),
        scratch_shapes=list(scratch),
        compiler_params=pltpu.CompilerParams(vmem_limit_bytes=VMEM_BYTES),
        cost_estimate=NO_COST,
    )(*operands)


def shape_of(rows, cols, dtype=BF):
    return jax.ShapeDtypeStruct((rows, cols), dtype)


def piece_rows(j, rows, i, size):
    if isinstance(i, int):
        return pl.ds(j * rows + i * size, size)
    return pl.ds(pl.multiple_of(j * rows + i * size, size), size)


def conv_block(starts, offset, pieces, taps, point, ring_rows, group):
    count = len(pieces)
    rows = pieces[0].shape[0]
    length, channels = rows * count, pieces[0].shape[1]
    inner = point.shape[0]

    def kernel(*refs):
        starts_ref, offset_ref = refs[:2]
        ins = refs[2 : 2 + count]
        taps_ref, point_ref = refs[2 + count : 4 + count]
        pre_ref = refs[4 + count]
        parts = refs[5 + count : 5 + 2 * count]
        sent = refs[5 + 2 * count : 5 + 2 * count + group]
        act, wide, prod, mid = refs[5 + 2 * count + group :]
        size = row_chunk(rows)
        for j in range(count):

            def body(i, j=j):
                x = ins[j][rows_at(i, size), :].astype(F32)
                a = gelu(x * rms_scale(x)).astype(BF)
                here = piece_rows(j, rows, i, size)
                act[here, :] = a
                wide[:, here] = a.T

            loop_chunks(rows // size, body)
        big = min(256, length)

        def product(i):
            here = rows_at(i, big)
            prod[here, :] = dot_nt(act[here, :], taps_ref[...])

        loop_chunks(length // big, product)
        pre = shifted_sum(
            prod[:, :inner], prod[:, inner : 2 * inner], prod[:, 2 * inner :], offset_ref[0]
        )
        pre_ref[...] = pre
        middle = gelu(pre).astype(BF)
        mid[...] = middle
        for j in range(count):

            def back(i, j=j):
                here = piece_rows(j, rows, i, size)
                parts[j][rows_at(i, size), :] = dot_nn(mid[here, :], point_ref[...]).astype(BF)

            loop_chunks(rows // size, back)
        emit_rows(starts_ref, wide, sent, ring_rows)
        for out in sent:
            out[ring_rows:, :] = middle.T

    outs = [shape_of(length, inner, F32)] + [shape_of(rows, channels)] * count
    outs += [shape_of(ring_rows + inner, length)] * group
    scratch = [
        pltpu.VMEM((length, channels), BF),
        pltpu.VMEM((channels, length), BF),
        pltpu.VMEM((length, 3 * inner), F32),
        pltpu.VMEM((length, inner), BF),
    ]
    res = call(kernel, outs, [starts, offset, *pieces, taps, point], 2, scratch)
    return res[0], res[1 : 1 + count], res[1 + count :]


def norm_block(near, cross, pieces, parts, moved, ring_rows, group):
    count = len(pieces)
    rows, channels = pieces[0].shape
    length = rows * count

    def kernel(*refs):
        near_ref, cross_ref = refs[:2]
        ins = refs[2 : 2 + count]
        firsts = refs[2 + count : 2 + 2 * count]
        adds = refs[2 + 2 * count : 2 + 2 * count + len(moved)]
        rest = refs[2 + 2 * count + len(moved) :]
        res_ref, norm_ref = rest[:2]
        sent = rest[2 : 2 + 2 * group]
        wide = rest[2 + 2 * group]
        size = row_chunk(rows)
        for j in range(count):

            def body(i, j=j):
                here = piece_rows(j, rows, i, size)
                total = firsts[j][rows_at(i, size), :].astype(F32)
                if adds:
                    total = total + adds[j][rows_at(i, size), :].astype(F32)
                res = (ins[j][rows_at(i, size), :].astype(F32) + total).astype(BF)
                res_ref[here, :] = res
                res = res.astype(F32)
                a = (res * rms_scale(res)).astype(BF)
                norm_ref[here, :] = a
                wide[:, here] = a.T

            loop_chunks(rows // size, body)
        emit_rows(near_ref, wide, sent[:group], ring_rows)
        emit_rows(cross_ref, wide, sent[group:], ring_rows)

    outs = [shape_of(length, channels), shape_of(length, channels)]
    outs += [shape_of(ring_rows, length)] * (2 * group)
    scratch = [pltpu.VMEM((channels, length), BF)]
    res = call(kernel, outs, [near, cross, *pieces, *parts, *moved], 2, scratch)
    return res[0], res[1], res[2 : 2 + group], res[2 + group :]


def widen_block(starts, pieces, ring_rows, group):
    count = len(pieces)
    rows, channels = pieces[0].shape
    length = rows * count

    def kernel(*refs):
        starts_ref = refs[0]
        ins = refs[1 : 1 + count]
        whole_ref = refs[1 + count]
        sent = refs[2 + count : 2 + count + group]
        wide = refs[2 + count + group]
        size = row_chunk(rows)
        for j in range(count):

            def body(i, j=j):
                here = piece_rows(j, rows, i, size)
                a = ins[j][rows_at(i, size), :]
                whole_ref[here, :] = a
                wide[:, here] = a.T

            loop_chunks(rows // size, body)
        emit_rows(starts_ref, wide, sent, ring_rows)

    outs = [shape_of(length, channels)] + [shape_of(ring_rows, length)] * group
    scratch = [pltpu.VMEM((channels, length), BF)]
    res = call(kernel, outs, [starts, *pieces], 1, scratch)
    return res[0], res[1:]


def attention_block(normed, grad_y, query_w, key_w, value_w, out_w, count):
    length, channels = normed.shape
    rows = length // count
    features = query_w.shape[0]
    heads = features // HSIZE
    per_step = 2 if heads % 2 == 0 else 1
    width = per_step * HSIZE
    inv_root = 1.0 / math.sqrt(HSIZE)
    chunk = min(256, length)

    def kernel(n_ref, gy_ref, wq, wk, wv, wo, qk_ref, va_ref, *rest):
        dns, acc = rest[:count], rest[count]
        step = pl.program_id(0)
        n = n_ref[...]
        gy = gy_ref[...]
        dqs, dks, dvs, ats = [], [], [], []
        for h in range(per_step):
            head = pl.ds(h * HSIZE, HSIZE)
            q = dot_nt(n, wq[head, :]).astype(BF)
            k = dot_nt(n, wk[head, :]).astype(BF)
            v = dot_nt(n, wv[head, :]).astype(BF)
            g = dot_nt(gy, wo[head, :]).astype(BF)
            dq, at = [], []
            dk = dv = None
            for c in range(length // chunk):
                qc = q[c * chunk : (c + 1) * chunk]
                gc = g[c * chunk : (c + 1) * chunk]
                ratio = jnp.tanh(dot_nt(qc, k) * (inv_root / SOFT_CAP))
                unnormed = jnp.exp(SOFT_CAP * ratio)
                soft = unnormed / jnp.sum(unnormed, axis=-1, keepdims=True)
                low = soft.astype(BF)
                at.append(dot_nn(low, v))
                gs = dot_nt(gc, v)
                gs = soft * (gs - jnp.sum(soft * gs, axis=-1, keepdims=True))
                gs = (gs * (1.0 - ratio * ratio)).astype(BF)
                dq.append(dot_nn(gs, k) * inv_root)
                dk_c = dot_tn(gs, qc)
                dv_c = dot_tn(low, gc)
                dk = dk_c if dk is None else dk + dk_c
                dv = dv_c if dv is None else dv + dv_c
            join = (lambda parts: parts[0] if len(parts) == 1 else jnp.concatenate(parts, axis=0))
            dqs.append(join(dq))
            ats.append(join(at))
            dks.append(dk * inv_root)
            dvs.append(dv)
        side = (lambda parts: parts[0] if len(parts) == 1 else jnp.concatenate(parts, axis=1))
        dq, dk, dv, at = [side(t).astype(BF) for t in (dqs, dks, dvs, ats)]
        qk_ref[0] = dq
        qk_ref[1] = dk
        va_ref[0] = dv
        va_ref[1] = at
        total = dot_nn(dq, wq[...]) + dot_nn(dk, wk[...]) + dot_nn(dv, wv[...])

        @pl.when(step == 0)
        def _():
            acc[...] = total

        @pl.when(step > 0)
        def _():
            acc[...] += total

        @pl.when(step == pl.num_programs(0) - 1)
        def _():
            for j in range(count):
                dns[j][...] = acc[pl.ds(j * rows, rows), :].astype(BF)

    whole = pl.BlockSpec((length, channels), lambda i: (0, 0))
    weight = pl.BlockSpec((width, channels), lambda i: (i, 0))
    column = pl.BlockSpec((2, length, width), lambda i: (0, 0, i))
    piece = pl.BlockSpec((rows, channels), lambda i: (0, 0))
    return pl.pallas_call(
        kernel,
        grid=(heads // per_step,),
        out_shape=[jax.ShapeDtypeStruct((2, length, features), BF)] * 2
        + [shape_of(rows, channels)] * count,
        in_specs=[whole, whole, weight, weight, weight, weight],
        out_specs=[column] * 2 + [piece] * count,
        scratch_shapes=[pltpu.VMEM((length, channels), F32)],
        compiler_params=pltpu.CompilerParams(vmem_limit_bytes=VMEM_BYTES),
        cost_estimate=NO_COST,
    )(normed, grad_y, query_w, key_w, value_w, out_w)


def back_block(starts, residual, grad_y, parts, moved, pre, point, ring_rows, group):
    length, channels = residual.shape
    inner = point.shape[0]
    count = len(parts)
    rows = length // count

    def kernel(*refs):
        starts_ref, res_ref, gy_ref = refs[:3]
        firsts = refs[3 : 3 + count]
        adds = refs[3 + count : 3 + count + len(moved)]
        pre_ref, point_ref = refs[3 + count + len(moved) : 5 + count + len(moved)]
        rest = refs[5 + count + len(moved) :]
        gc_ref = rest[0]
        sent = rest[1 : 1 + group]
        wide, resid_grad = rest[1 + group :]
        size = row_chunk(rows)
        for j in range(count):

            def body(i, j=j):
                here = piece_rows(j, rows, i, size)
                gn = firsts[j][rows_at(i, size), :].astype(F32)
                if adds:
                    gn = gn + adds[j][rows_at(i, size), :].astype(F32)
                res = res_ref[here, :].astype(F32)
                scale = rms_scale(res)
                inner_mean = jnp.mean(gn * res, axis=-1, keepdims=True)
                a = gy_ref[here, :].astype(F32) + (
                    scale * gn - res * (scale * scale * scale) * inner_mean
                )
                a = a.astype(BF)
                resid_grad[here, :] = a
                wide[:, here] = a.T

            loop_chunks(rows // size, body)
        big = min(256, length)

        def product(i):
            here = rows_at(i, big)
            gm = dot_nt(resid_grad[here, :], point_ref[...])
            gc_ref[here, :] = (gelu_slope(pre_ref[here, :]) * gm).astype(BF)

        loop_chunks(length // big, product)
        emit_rows(starts_ref, wide, sent, ring_rows)

    outs = [shape_of(length, inner)] + [shape_of(ring_rows, length)] * group
    scratch = [pltpu.VMEM((channels, length), BF), pltpu.VMEM((length, channels), BF)]
    res = call(
        kernel,
        outs,
        [starts, residual, grad_y, *parts, *moved, pre, point],
        1,
        scratch,
    )
    return res[0], res[1:]


def store_halves(outs, total, side, cols):
    half = total.shape[0] // len(outs)
    for k, out in enumerate(outs):
        part = total[k * half : (k + 1) * half]
        out[:, side * cols : (side + 1) * cols] = part


def pair_sum(first_wides, second_wides, narrows, halves):
    group = len(first_wides)
    rows, length = first_wides[0].shape
    cols = narrows[0].shape[2]
    same = first_wides is second_wides
    wides = first_wides if same else first_wides + second_wides

    def kernel(*refs):
        a_refs, b_refs = refs[: len(wides)], refs[len(wides) : len(wides) + group]
        outs = refs[len(wides) + group :]
        for side in range(2):
            total = None
            for p in range(group):
                a = a_refs[p if same else side * group + p][...]
                term = dot_nn(a, b_refs[p][side])
                total = term if total is None else total + term
            store_halves(outs, total.astype(BF), side, cols)

    return call(kernel, [shape_of(rows // halves, 2 * cols)] * halves, [*wides, *narrows], 0)


def tap_sum(offset, packs, conv_narrows, halves, rows):
    group = len(packs)
    length, inner = conv_narrows[0].shape
    step = DILATION_STEP

    def kernel(offset_ref, *refs):
        pack_refs, conv_refs = refs[:group], refs[group : 2 * group]
        outs = refs[2 * group :]
        pos = lax.rem(lax.broadcasted_iota(jnp.int32, (length, 1), 0) + offset_ref[0], length)
        total = [None] * 3
        for p in range(group):
            a = pack_refs[p][:rows, :]
            b = conv_refs[p][...]
            up = jnp.concatenate([b[step:], b[:step]], axis=0).astype(F32)
            down = jnp.concatenate([b[length - step :], b[: length - step]], axis=0).astype(F32)
            first = jnp.where(pos < length - step, up, 0.0).astype(BF)
            last = jnp.where(pos >= step, down, 0.0).astype(BF)
            terms = [dot_nn(a, moved) for moved in (first, b, last)]
            total = [t if old is None else old + t for old, t in zip(total, terms)]
        for side in range(3):
            store_halves(outs, total[side].astype(BF), side, inner)

    outs = [shape_of(rows // halves, 3 * inner)] * halves
    return call(kernel, outs, [offset, *packs, *conv_narrows], 1)


def point_sum(packs, resid_wides, halves):
    group = len(packs)
    rows = resid_wides[0].shape[0]
    inner = packs[0].shape[0] - rows

    def kernel(*refs):
        pack_refs, wide_refs = refs[:group], refs[group : 2 * group]
        total = None
        for p in range(group):
            term = dot_nt(wide_refs[p][...], pack_refs[p][rows:, :])
            total = term if total is None else total + term
        store_halves(refs[2 * group :], total.astype(BF), 0, inner)

    outs = [shape_of(rows // halves, inner)] * halves
    return call(kernel, outs, [*packs, *resid_wides], 0)


def after(value, *others):
    return lax.optimization_barrier((value, others))[0]


def shards(
    inputs,
    dilated_tap_weight,
    point_weight,
    query_weight,
    key_weight,
    value_weight,
    out_weight,
    cotangent,
):
    channels = inputs.shape[2]
    own = inputs[0]
    rows = own.shape[0]
    n_seq = lax.axis_size("seq")
    n_dp = lax.axis_size("dp")
    length = rows * n_seq
    pair = n_seq == 2
    block = channels // n_dp
    inner = point_weight.shape[0]
    features = query_weight.shape[0]
    inv_tokens = 1.0 / math.sqrt(inputs.shape[0] * n_dp * length)

    bits = [1 << i for i in range(n_dp.bit_length() - 1)]
    near_bits, near_rest = bits[:2], bits[2:]
    if len(bits) > 2:
        cross_bits, cross_rest = [bits[0], bits[2]], [bits[1], *bits[3:]]
    else:
        cross_bits, cross_rest = near_bits, near_rest
    group = 1 << len(near_bits)
    ring_rows = channels // group
    halves = 2 if near_rest else 1

    me_dp = lax.axis_index("dp")
    me_seq = lax.axis_index("seq")

    def combos(of):
        found = [0]
        for bit in of:
            found += [value | bit for value in found]
        return found

    def starts_of(peers, rest):
        order = combos(rest[::-1])
        places = [peer ^ k for peer in combos(peers) for k in order]
        return ((me_dp ^ jnp.array(places, jnp.int32)) * block).astype(jnp.int32)

    near = starts_of(near_bits, near_rest)
    cross = starts_of(cross_bits, cross_rest)
    offset = (me_seq * rows if pair else jnp.int32(0)).astype(jnp.int32).reshape(1)

    def swap_seq(x):
        return lax.ppermute(x, "seq", [(0, 1), (1, 0)])

    def to_peer(x, bit):
        if bit == 0:
            return x
        return lax.ppermute(x, "dp", [(i, i ^ bit) for i in range(n_dp)])

    def gather_seq(x):
        if pair:
            return [x, swap_seq(x)]
        return [lax.all_gather(x, "seq", axis=0, tiled=True)]

    def add_seq(parts):
        if pair:
            return parts, [swap_seq(parts[1]), swap_seq(parts[0])]
        summed = lax.psum_scatter(parts[0], "seq", scatter_dimension=0, tiled=True)
        return [lax.all_gather(summed, "seq", axis=0, tiled=True)], []

    def share_wide(pieces, peers):
        return [to_peer(piece, p) for piece, p in zip(pieces, combos(peers))]

    def send_narrow(x, peers):
        return [x] + [to_peer(x, bit) for bit in peers]

    def pass_narrow(got, peers):
        return got + [to_peer(got[2], peers[0])] if len(peers) == 2 else got

    def first_half(totals, rest):
        return to_peer(totals[1], rest[0]) if rest else None

    def add_half(totals, got):
        kept = totals[0].astype(F32)
        return kept if got is None else kept + got.astype(F32)

    def later_halves(kept, rest):
        for bit in rest[1:]:
            half = kept.shape[0] // 2
            got = to_peer(kept[half:].astype(BF), bit)
            kept = kept[:half] + got.astype(F32)
        return kept

    pieces = gather_seq(own)
    grad_own = (cotangent[0].astype(F32) * inv_tokens).astype(BF)
    taps = dilated_tap_weight.reshape(3 * inner, channels)
    pre, parts, packs = conv_block(near, offset, pieces, taps, point_weight, ring_rows, group)
    grad_pieces = gather_seq(grad_own)
    parts, moved = add_seq(parts)
    packs = share_wide(packs, near_bits)
    grad_y, grad_sent = widen_block(cross, grad_pieces, ring_rows, group)
    grad_cross = share_wide(grad_sent, cross_bits)
    moved = after(moved, packs)
    residual, normed, norm_near, norm_cross = norm_block(
        near, cross, pieces, parts, moved, ring_rows, group
    )
    norm_near = share_wide(norm_near, near_bits)
    norm_cross = share_wide(norm_cross, cross_bits)

    delta_qk, delta_va, *grad_parts = attention_block(
        normed, grad_y, query_weight, key_weight, value_weight, out_weight, len(pieces)
    )
    grad_parts, delta_qk, delta_va, norm_near, norm_cross, grad_cross = lax.optimization_barrier(
        (grad_parts, delta_qk, delta_va, norm_near, norm_cross, grad_cross)
    )
    grad_parts, grad_moved = add_seq(grad_parts)
    qk_all = send_narrow(delta_qk, near_bits)
    va_all = send_narrow(delta_va, cross_bits)
    attn_part = dot_nn(delta_va[1], out_weight).astype(BF)
    grad_moved = after(grad_moved, qk_all, va_all)
    grad_conv, resid_sent = back_block(
        near, residual, grad_y, grad_parts, grad_moved, pre, point_weight, ring_rows, group
    )
    conv_all = send_narrow(grad_conv, near_bits)
    qk_all = pass_narrow(after(qk_all, grad_conv), near_bits)
    va_all = pass_narrow(after(va_all, grad_conv), cross_bits)
    resid_near = share_wide(resid_sent, near_bits)
    attn_part = after(attn_part, grad_conv)
    if pair:
        attn_rows = attn_part[:rows].astype(F32) + swap_seq(attn_part[rows:]).astype(F32)
        res_own = residual[:rows]
    else:
        attn_rows = lax.psum_scatter(attn_part, "seq", scatter_dimension=0, tiled=True)
        attn_rows = attn_rows.astype(F32)
        res_own = lax.dynamic_slice_in_dim(residual, me_seq * rows, rows, 0)
    output = (res_own.astype(F32) + attn_rows).astype(BF)[None]

    qk_total = pair_sum(norm_near, norm_near, qk_all, halves)
    qk_got = first_half(qk_total, near_rest)
    conv_all = pass_narrow(after(conv_all, qk_total), near_bits)
    tap_total = tap_sum(offset, packs, conv_all, halves, ring_rows)
    tap_got = first_half(tap_total, near_rest)
    va_total = pair_sum(norm_cross, grad_cross, after(va_all, tap_total), halves)
    va_got = first_half(va_total, cross_rest)
    point_total = point_sum(packs, after(resid_near, va_total), halves)
    point_got = first_half(point_total, near_rest)

    qk_kept = add_half(qk_total, after(qk_got, point_total))
    tap_kept = add_half(tap_total, after(tap_got, qk_kept))
    va_kept = add_half(va_total, after(va_got, tap_kept))
    point_kept = add_half(point_total, after(point_got, va_kept))
    qk_done = later_halves(qk_kept, near_rest)
    tap_done = later_halves(tap_kept, near_rest)
    va_done = later_halves(va_kept, cross_rest)
    point_done = later_halves(point_kept, near_rest)
    return (
        output,
        tap_done.reshape(block, 3, inner).transpose(1, 0, 2),
        point_done.T,
        qk_done[:, :features],
        qk_done[:, features:],
        va_done[:, :features],
        va_done[:, features:].T,
    )


def solution(mesh):
    placed = (
        P("dp", "seq", None),
        P(None, "seq", None),
        P("seq", None),
        P("seq", None),
        P("seq", None),
        P("seq", None),
        P("seq", None),
        P("dp", "seq", None),
    )
    return jax.shard_map(
        shards,
        mesh=mesh,
        in_specs=placed,
        out_specs=(
            P("dp", "seq", None),
            P(None, "dp", "seq"),
            P("seq", "dp"),
            P("dp", "seq"),
            P("dp", "seq"),
            P("dp", "seq"),
            P("seq", "dp"),
        ),
        check_vma=False,
    )
```

```python
import functools
import math

import jax
import jax.numpy as jnp
from jax import lax
from jax.experimental import pallas as pl
from jax.experimental.pallas import tpu as pltpu
from jax.sharding import PartitionSpec as P

HSIZE = 192
DILATION_STEP = 16
EPSILON = 1e-06
SOFT_CAP = 6.0
GELU_C = math.sqrt(2.0 / math.pi)
GELU_A = 0.044715
BF = jnp.bfloat16
F32 = jnp.float32
ORDER = (
    "q_sum", "mm", "v_sum", "back", "q_add", "k_sum", "tap_sum", "q_end", "v_add", "k_add", "o_sum",
    "v_end", "point_sum", "tap_add", "k_end", "o_add", "point_add", "tap_end", "o_end", "point_end",
)
SENDS = (
    ("q_far", "start"), ("v_far", "start"), ("k_far", "q_far"), ("wides", "near"),
    ("q_pass", "start"), ("v_pass", "start"), ("tap_far", "back"), ("resid_far", "tap_far"),
    ("k_pass", "back"), ("o_far", "back"), ("tap_pass", "back"), ("olds", "back"),
    ("o_pass", "tap_sum"), ("point_pass", "tap_sum"),
)
NEEDED = ("q_got",)
NO_COST = pl.CostEstimate(flops=0, bytes_accessed=0, transcendentals=0)


def gelu(x):
    return 0.5 * x * (1.0 + jnp.tanh(GELU_C * (x + GELU_A * (x * x * x))))


def gelu_slope(x):
    t = jnp.tanh(GELU_C * (x + GELU_A * (x * x * x)))
    return 0.5 * (1.0 + t) + 0.5 * x * (1.0 - t * t) * GELU_C * (1.0 + 3.0 * GELU_A * x * x)


def dot_nn(a, b):
    return lax.dot_general(a, b, (((1,), (0,)), ((), ())), preferred_element_type=F32)


def dot_nt(a, b):
    return lax.dot_general(a, b, (((1,), (1,)), ((), ())), preferred_element_type=F32)


def dot_tn(a, b):
    return lax.dot_general(a, b, (((0,), (0,)), ((), ())), preferred_element_type=F32)


def rms_scale(x):
    return lax.rsqrt(jnp.mean(x * x, axis=-1, keepdims=True) + EPSILON)


def row_chunk(rows):
    return 128 if rows % 128 == 0 else rows


def loop_chunks(count, body):
    if count <= 2:
        for i in range(count):
            body(i)
    else:

        def step(i, carry):
            body(i)
            return carry

        lax.fori_loop(0, count, step, 0)


def rows_at(i, size):
    if isinstance(i, int):
        return pl.ds(i * size, size)
    return pl.ds(pl.multiple_of(i * size, size), size)


def emit_rows(starts, wide, outs, rows):
    peers = len(outs) if len(outs) < 3 else 4
    parts = starts.shape[0] // peers
    size = rows // parts
    for p in range(peers):
        out, base = (outs[2], (p - 2) * rows) if p > 1 else (outs[p], 0)
        for k in range(parts):
            at = pl.multiple_of(starts[p * parts + k], 16)
            out[base + k * size : base + (k + 1) * size, :] = wide[pl.ds(at, size), :]


def wide_shapes(group, rows, length, extra=0):
    found = [shape_of(rows + extra, length)] * min(group, 2)
    return found + [shape_of(2 * rows + extra, length)] * (group > 2)


def shifted_sum(first, middle, last, offset):
    length = middle.shape[0]
    step = DILATION_STEP
    pos = lax.rem(lax.broadcasted_iota(jnp.int32, (length, 1), 0) + offset, length)
    down = jnp.concatenate([first[length - step :], first[: length - step]], axis=0)
    up = jnp.concatenate([last[step:], last[:step]], axis=0)
    return jnp.where(pos >= step, down, 0.0) + middle + jnp.where(pos < length - step, up, 0.0)


def vmem_params(arrays, copies=1):
    held = sum(math.prod(t.shape) * jnp.dtype(t.dtype).itemsize for t in arrays)
    return pltpu.CompilerParams(vmem_limit_bytes=min(56 << 20, copies * held + (8 << 20)))


def call(kernel, out_shape, operands, smem=1, scratch=()):
    specs = [pl.BlockSpec(memory_space=pltpu.SMEM)] * smem
    specs += [pl.BlockSpec(memory_space=pltpu.VMEM)] * (len(operands) - smem)
    return pl.pallas_call(
        kernel,
        out_shape=out_shape,
        in_specs=specs,
        out_specs=[pl.BlockSpec(memory_space=pltpu.VMEM)] * len(out_shape),
        scratch_shapes=list(scratch),
        compiler_params=vmem_params([*operands, *out_shape, *scratch]),
        cost_estimate=NO_COST,
    )(*operands)


def shape_of(rows, cols, dtype=BF):
    return jax.ShapeDtypeStruct((rows, cols), dtype)


def parts_shape(count, rows, cols):
    return jax.ShapeDtypeStruct((count, rows, cols), BF)


def store_parts(parts_ref, place, value):
    rows, size = parts_ref.shape[1], value.shape[0]
    for at in range(0, size, min(rows, size)):
        j, first = divmod(place * size + at, rows)
        parts_ref[j, first : first + min(rows, size), :] = value[at : at + min(rows, size)]


def summed_rows(parts_ref, moved, j, here):
    total = parts_ref[j, here, :].astype(F32)
    for ref in moved:
        total = total + ref[1 - j, here, :].astype(F32)
    return total


def piece_rows(j, rows, i, size):
    if isinstance(i, int):
        return pl.ds(j * rows + i * size, size)
    return pl.ds(pl.multiple_of(j * rows + i * size, size), size)


def scaled_rows(rows, factor, *ahead):
    def kernel(*refs):
        refs[-1][...] = (refs[0][...].astype(F32) * factor).astype(BF)

    return call(kernel, [shape_of(*rows.shape)], [rows, *ahead], 0)[0]


def conv_block(offset, pieces, taps, point):
    count = len(pieces)
    rows, channels = pieces[0].shape
    length = rows * count
    inner = point.shape[0]

    def kernel(*refs):
        offset_ref, ins = refs[0], refs[1 : 1 + count]
        taps_ref, point_ref, pre_ref, parts_ref, mid_ref, act_ref, prod = refs[1 + count :]
        size = row_chunk(rows)
        for j in range(count):

            def body(i, j=j):
                x = ins[j][rows_at(i, size), :].astype(F32)
                act_ref[piece_rows(j, rows, i, size), :] = gelu(x * rms_scale(x)).astype(BF)

            loop_chunks(rows // size, body)
        big = min(256, length)

        def product(i):
            here = rows_at(i, big)
            prod[here, :] = dot_nt(act_ref[here, :], taps_ref[...])

        loop_chunks(length // big, product)
        pre = shifted_sum(
            prod[:, :inner], prod[:, inner : 2 * inner], prod[:, 2 * inner :], offset_ref[0]
        )
        pre_ref[...] = pre
        mid_ref[...] = gelu(pre).astype(BF)
        for c in range(length // big):
            total = dot_nn(mid_ref[c * big : (c + 1) * big, :], point_ref[...])
            store_parts(parts_ref, c, total.astype(BF))

    outs = [
        shape_of(length, inner, F32),
        parts_shape(count, rows, channels),
        shape_of(length, inner),
        shape_of(length, channels),
    ]
    scratch = [pltpu.VMEM((length, 3 * inner), F32)]
    return call(kernel, outs, [offset, *pieces, taps, point], 1, scratch)


def pack_block(starts, act, middle, ring_rows, group):
    length, inner = middle.shape
    channels = act.shape[1]

    def kernel(*refs):
        starts_ref, act_ref, mid_ref = refs[:3]
        sent, wide = refs[3:-1], refs[-1]
        size = row_chunk(length)

        def body(i):
            here = rows_at(i, size)
            wide[:, here] = act_ref[here, :].T

        loop_chunks(length // size, body)
        emit_rows(starts_ref, wide, sent, ring_rows)
        turned = mid_ref[...].T
        for out in sent:
            out[out.shape[0] - inner :, :] = turned

    outs = wide_shapes(group, ring_rows, length, inner)
    scratch = [pltpu.VMEM((channels, length), BF)]
    return call(kernel, outs, [starts, act, middle], 1, scratch)


def head_grads(grad_y, out_w):
    def kernel(gy_ref, wo_ref, out_ref):
        out_ref[...] = dot_nt(gy_ref[...], wo_ref[...]).astype(BF)

    return call(kernel, [shape_of(grad_y.shape[0], out_w.shape[0])], [grad_y, out_w], 0)[0]


def norm_block(near, cross, pieces, parts, moved, ring_rows, group):
    count = len(pieces)
    rows, channels = pieces[0].shape
    length = rows * count

    def kernel(*refs):
        near_ref, cross_ref = refs[:2]
        ins = refs[2 : 2 + count]
        parts_ref = refs[2 + count]
        adds = refs[3 + count : 3 + count + len(moved)]
        rest = refs[3 + count + len(moved) :]
        res_ref, norm_ref = rest[:2]
        sent, wide = rest[2:-1], rest[-1]
        size = row_chunk(rows)
        for j in range(count):

            def body(i, j=j):
                here = piece_rows(j, rows, i, size)
                total = summed_rows(parts_ref, adds, j, rows_at(i, size))
                res = (ins[j][rows_at(i, size), :].astype(F32) + total).astype(BF)
                res_ref[here, :] = res
                res = res.astype(F32)
                a = (res * rms_scale(res)).astype(BF)
                norm_ref[here, :] = a
                wide[:, here] = a.T

            loop_chunks(rows // size, body)
        emit_rows(near_ref, wide, sent[: len(sent) // 2], ring_rows)
        emit_rows(cross_ref, wide, sent[len(sent) // 2 :], ring_rows)

    outs = [shape_of(length, channels), shape_of(length, channels)]
    sides = wide_shapes(group, ring_rows, length)
    outs += sides + sides
    scratch = [pltpu.VMEM((channels, length), BF)]
    res = call(kernel, outs, [near, cross, *pieces, parts, *moved], 2, scratch)
    return res[0], res[1], res[2 : 2 + len(sides)], res[2 + len(sides) :]


def widen_block(starts, pieces, ring_rows, group):
    count = len(pieces)
    rows, channels = pieces[0].shape
    length = rows * count

    def kernel(*refs):
        starts_ref = refs[0]
        ins = refs[1 : 1 + count]
        whole_ref = refs[1 + count]
        sent, wide = refs[2 + count : -1], refs[-1]
        size = row_chunk(rows)
        for j in range(count):

            def body(i, j=j):
                here = piece_rows(j, rows, i, size)
                a = ins[j][rows_at(i, size), :]
                whole_ref[here, :] = a
                wide[:, here] = a.T

            loop_chunks(rows // size, body)
        emit_rows(starts_ref, wide, sent, ring_rows)

    outs = [shape_of(length, channels)] + wide_shapes(group, ring_rows, length)
    scratch = [pltpu.VMEM((channels, length), BF)]
    res = call(kernel, outs, [starts, *pieces], 1, scratch)
    return res[0], res[1:]


def attention_block(normed, grad_heads, query_w, key_w, value_w, count):
    length, channels = normed.shape
    rows = length // count
    features = query_w.shape[0]
    heads = features // HSIZE
    joined = 2 if heads % 2 == 0 else 1
    inv_root = 1.0 / math.sqrt(HSIZE)
    chunk = min(256, length)

    def one_head(q, k, v, g):
        dq, at = [], []
        dk = dv = None
        for c in range(length // chunk):
            qc = q[c * chunk : (c + 1) * chunk]
            gc = g[c * chunk : (c + 1) * chunk]
            ratio = jnp.tanh(dot_nt(qc, k) * (inv_root / SOFT_CAP))
            unnormed = jnp.exp(SOFT_CAP * ratio)
            soft = unnormed / jnp.sum(unnormed, axis=-1, keepdims=True)
            low = soft.astype(BF)
            at.append(dot_nn(low, v))
            gs = dot_nt(gc, v)
            gs = soft * (gs - jnp.sum(soft * gs, axis=-1, keepdims=True))
            gs = (gs * (1.0 - ratio * ratio)).astype(BF)
            dq.append(dot_nn(gs, k) * inv_root)
            dk_c = dot_tn(gs, qc)
            dv_c = dot_tn(low, gc)
            dk = dk_c if dk is None else dk + dk_c
            dv = dv_c if dv is None else dv + dv_c
        return side(dq, 0), dk * inv_root, dv, side(at, 0)

    def side(parts, axis):
        return parts[0] if len(parts) == 1 else jnp.concatenate(parts, axis=axis)

    def kernel(n_ref, gh_ref, wq, wk, wv, *rest):
        refs, all_ref, dn_ref = rest[:4], rest[4], rest[5]
        q_ref, k_ref, v_ref = rest[6:]

        def project(i):
            here = rows_at(i, chunk)
            n = n_ref[here, :]
            for w, ref in ((wq, q_ref), (wk, k_ref), (wv, v_ref)):
                ref[here, :] = dot_nt(n, w[...]).astype(BF)

        loop_chunks(length // chunk, project)
        for h in range(0, heads, joined):
            found = []
            for m in range(h, h + joined):
                cols = slice(m * HSIZE, (m + 1) * HSIZE)
                found.append(
                    one_head(q_ref[:, cols], k_ref[:, cols], v_ref[:, cols], gh_ref[:, cols])
                )
            cols = slice(h * HSIZE, (h + joined) * HSIZE)
            for place, ref in enumerate(refs):
                value = side([t[place] for t in found], 1).astype(BF)
                ref[:, cols] = value
                all_ref[place, :, cols] = value
        for c in range(length // chunk):
            here = pl.ds(c * chunk, chunk)
            total = None
            for ref, w in zip(refs, (wq, wk, wv)):
                term = dot_nn(ref[here, :], w[...])
                total = term if total is None else total + term
            store_parts(dn_ref, c, total.astype(BF))

    outs = [shape_of(length, features)] * 4
    outs += [parts_shape(4, length, features), parts_shape(count, rows, channels)]
    scratch = [pltpu.VMEM((length, features), BF)] * 3
    return call(kernel, outs, [normed, grad_heads, query_w, key_w, value_w], 0, scratch)


def back_block(starts, residual, grad_y, parts, moved, pre, point, ring_rows, group):
    length, channels = residual.shape
    inner = point.shape[0]
    count, rows = parts.shape[:2]

    def kernel(*refs):
        starts_ref, res_ref, gy_ref, parts_ref = refs[:4]
        adds = refs[4 : 4 + len(moved)]
        pre_ref, point_ref = refs[4 + len(moved) : 6 + len(moved)]
        rest = refs[6 + len(moved) :]
        gc_ref = rest[0]
        sent = rest[1:-2]
        wide, resid_grad = rest[-2:]
        size = row_chunk(rows)
        for j in range(count):

            def body(i, j=j):
                here = piece_rows(j, rows, i, size)
                gn = summed_rows(parts_ref, adds, j, rows_at(i, size))
                res = res_ref[here, :].astype(F32)
                scale = rms_scale(res)
                inner_mean = jnp.mean(gn * res, axis=-1, keepdims=True)
                a = gy_ref[here, :].astype(F32) + (
                    scale * gn - res * (scale * scale * scale) * inner_mean
                )
                a = a.astype(BF)
                resid_grad[here, :] = a
                wide[:, here] = a.T

            loop_chunks(rows // size, body)
        big = min(256, length)

        def product(i):
            here = rows_at(i, big)
            gm = dot_nt(resid_grad[here, :], point_ref[...])
            gc_ref[here, :] = (gelu_slope(pre_ref[here, :]) * gm).astype(BF)

        loop_chunks(length // big, product)
        emit_rows(starts_ref, wide, sent, ring_rows)

    outs = [shape_of(length, inner)] + wide_shapes(group, ring_rows, length)
    scratch = [pltpu.VMEM((channels, length), BF), pltpu.VMEM((length, channels), BF)]
    res = call(
        kernel,
        outs,
        [starts, residual, grad_y, parts, *moved, pre, point],
        1,
        scratch,
    )
    return res[0], res[1:]


def store_halves(outs, total, side, cols):
    half = total.shape[0] // len(outs)
    for k, out in enumerate(outs):
        part = total[k * half : (k + 1) * half]
        out[:, side * cols : (side + 1) * cols] = part


def wide_rows(ref, place, rows):
    return ref[rows : 2 * rows, :] if place == 3 else ref[:rows, :]


def weight_sum(wides, narrows, place, halves):
    group = len(wides)
    rows = wides[0].shape[0]
    cols = narrows[0].shape[1]

    def kernel(*refs):
        total = None
        for p in range(group):
            b_ref = refs[group + p]
            b = b_ref[place] if len(b_ref.shape) == 3 else b_ref[...]
            term = dot_nn(wide_rows(refs[p], p, rows), b)
            total = term if total is None else total + term
        store_halves(refs[2 * group :], total.astype(BF), 0, cols)

    return call(kernel, [shape_of(rows // halves, cols)] * halves, [*wides, *narrows], 0)


def tap_sum(offset, packs, conv_narrows, halves, rows):
    group = len(packs)
    length, inner = conv_narrows[0].shape
    step = DILATION_STEP

    def kernel(offset_ref, *refs):
        pack_refs, conv_refs = refs[:group], refs[group : 2 * group]
        outs = refs[2 * group :]
        pos = lax.rem(lax.broadcasted_iota(jnp.int32, (length, 1), 0) + offset_ref[0], length)
        total = [None] * 3
        for p in range(group):
            a = wide_rows(pack_refs[p], p, rows)
            b = conv_refs[p][...]
            up = jnp.concatenate([b[step:], b[:step]], axis=0).astype(F32)
            down = jnp.concatenate([b[length - step :], b[: length - step]], axis=0).astype(F32)
            first = jnp.where(pos < length - step, up, 0.0).astype(BF)
            last = jnp.where(pos >= step, down, 0.0).astype(BF)
            terms = [dot_nn(a, moved) for moved in (first, b, last)]
            total = [t if old is None else old + t for old, t in zip(total, terms)]
        for side in range(3):
            store_halves(outs, total[side].astype(BF), side, inner)

    outs = [shape_of(rows // halves, 3 * inner)] * halves
    return call(kernel, outs, [offset, *packs, *conv_narrows], 1)


def point_sum(packs, resid_wides, halves):
    group = len(packs)
    rows = resid_wides[0].shape[0]
    inner = packs[0].shape[0] - rows

    def kernel(*refs):
        pack_refs, wide_refs = refs[:group], refs[group : 2 * group]
        total = None
        for p in range(group):
            middle = pack_refs[p][pack_refs[p].shape[0] - inner :, :]
            term = dot_nt(wide_rows(wide_refs[p], p, rows), middle)
            total = term if total is None else total + term
        store_halves(refs[2 * group :], total.astype(BF), 0, inner)

    outs = [shape_of(rows // halves, inner)] * halves
    return call(kernel, outs, [*packs, *resid_wides], 0)


def add_block(kept, got):
    rows, cols = kept.shape
    half = rows // 2

    def kernel(kept_ref, got_ref, first_ref, second_ref):
        first_ref[...] = kept_ref[:half, :].astype(F32) + got_ref[:half, :].astype(F32)
        second = kept_ref[half:, :].astype(F32) + got_ref[half:, :].astype(F32)
        second_ref[...] = second.astype(BF)

    return call(kernel, [shape_of(half, cols, F32), shape_of(half, cols)], [kept, got], 0)


def last_block(kept, got, form):
    rows, cols = kept.shape
    if form == "taps":
        out = jax.ShapeDtypeStruct((3, rows, cols // 3), F32)
    else:
        out = shape_of(rows, cols, F32)

    def kernel(*refs):
        total = refs[0][...].astype(F32)
        for ref in refs[1:-1]:
            total = total + ref[...].astype(F32)
        out_ref = refs[-1]
        if form == "taps":
            for k in range(3):
                out_ref[k] = total[:, k * (cols // 3) : (k + 1) * (cols // 3)]
        else:
            out_ref[...] = total

    return call(kernel, [out], [kept] if got is None else [kept, got], 0)[0]


def after(value, *others):
    return lax.optimization_barrier((value, others))[0]


def shards(
    inputs,
    dilated_tap_weight,
    point_weight,
    query_weight,
    key_weight,
    value_weight,
    out_weight,
    cotangent,
):
    channels = inputs.shape[2]
    own = inputs[0]
    rows = own.shape[0]
    n_seq = lax.axis_size("seq")
    n_dp = lax.axis_size("dp")
    length = rows * n_seq
    pair = n_seq == 2
    block = channels // n_dp
    inner = point_weight.shape[0]
    features = query_weight.shape[0]
    inv_tokens = 1.0 / math.sqrt(inputs.shape[0] * n_dp * length)

    bits = [1 << i for i in range(n_dp.bit_length() - 1)]
    near_bits, near_rest = bits[:2], bits[2:]
    cross_bits, cross_rest = near_bits, near_rest
    if len(bits) > 2:
        cross_bits, cross_rest = [bits[0], bits[2]], [bits[1], *bits[3:]]
    group = 1 << len(near_bits)
    ring_rows = channels // group
    halves = 2 if near_rest else 1

    me_dp = lax.axis_index("dp")
    me_seq = lax.axis_index("seq")

    def combos(of):
        found = [0]
        for bit in of:
            found += [value | bit for value in found]
        return found

    def starts_of(peers, rest):
        order = combos(rest[::-1])
        places = [peer ^ k for peer in combos(peers) for k in order]
        return ((me_dp ^ jnp.array(places, jnp.int32)) * block).astype(jnp.int32)

    near = starts_of(near_bits, near_rest)
    cross = starts_of(cross_bits, cross_rest)
    offset = (me_seq * rows if pair else jnp.int32(0)).astype(jnp.int32).reshape(1)

    def swap_seq(x):
        return lax.ppermute(x, "seq", [(0, 1), (1, 0)])

    def to_peer(x, bit):
        if bit == 0:
            return x
        return lax.ppermute(x, "dp", [(i, i ^ bit) for i in range(n_dp)])

    def gather_seq(x):
        if pair:
            return [x, swap_seq(x)]
        return [lax.all_gather(x, "seq", axis=0, tiled=True)]

    def add_seq(parts):
        if pair:
            return parts, [swap_seq(parts)]
        summed = lax.psum_scatter(parts[0], "seq", scatter_dimension=0, tiled=True)
        return lax.all_gather(summed, "seq", axis=0, tiled=True)[None], []

    def send_wide(pieces, peers):
        return [pieces[0]] + [to_peer(piece, p) for piece, p in zip(pieces[1:], peers)]

    def pass_on(got, peers):
        return list(got) + ([to_peer(got[2], peers[0])] if len(peers) > 1 else [])

    def send_far(x, peers):
        return to_peer(x, peers[1]) if len(peers) > 1 else None

    def gathered(x, near_copy, far_copy, peers):
        return pass_on([x, near_copy, far_copy][: 1 + len(peers)], peers)

    def send_half(totals, rest):
        return to_peer(totals[1], rest[0]) if rest else None

    def add_half(totals, got, rest):
        kept = totals[0]
        for bit in rest[1:]:
            kept, sent = add_block(kept, got)
            got = to_peer(sent, bit)
        return kept, got

    pieces = gather_seq(own)
    taps = dilated_tap_weight.reshape(3 * inner, channels)
    grad_own = scaled_rows(cotangent[0], inv_tokens, own, taps)
    grad_pieces = gather_seq(grad_own)
    pre, parts, middle, act = conv_block(offset, pieces, taps, point_weight)
    pre, parts, middle, act, grad_pieces = lax.optimization_barrier(
        (pre, parts, middle, act, grad_pieces)
    )
    parts, moved = add_seq(parts)
    packs = pack_block(near, act, middle, ring_rows, group)
    packs = send_wide(packs, near_bits)
    grad_y, grad_wide = widen_block(cross, grad_pieces, ring_rows, group)
    grad_wide = send_wide(grad_wide, cross_bits)
    grad_heads = head_grads(grad_y, out_weight)
    moved = after(moved, packs, grad_wide, grad_heads)
    residual, normed, norm_near, norm_cross = norm_block(
        near, cross, pieces, parts, moved, ring_rows, group
    )
    norm_near = send_wide(norm_near, near_bits)
    norm_cross = send_wide(norm_cross, cross_bits)

    *deltas, delta_all, grad_parts = attention_block(
        normed, grad_heads, query_weight, key_weight, value_weight, len(pieces)
    )
    grad_parts, deltas, delta_all, norm_near, norm_cross = lax.optimization_barrier(
        (grad_parts, deltas, delta_all, norm_near, norm_cross)
    )
    attended = deltas[3]
    grad_parts, grad_moved = add_seq(grad_parts)
    delta_near = to_peer(delta_all, bits[0]) if bits else None

    peers = {name: near_bits for name in ("q", "k", "tap", "point")}
    peers.update({name: cross_bits for name in ("v", "o")})
    rest = {name: cross_rest if peers[name] is cross_bits else near_rest for name in peers}
    place = {"q": 0, "k": 1, "v": 2, "o": 3}
    found = {}

    def wanted(value, *names):
        names = [name for name in names if name in found]
        return after(value, *[found[name] for name in names]) if names else value

    wides = {"q": norm_near, "k": norm_near, "v": norm_cross, "o": grad_wide, "tap": packs}

    def open_gates():
        for name, condition in SENDS:
            if name in found or condition not in found:
                continue
            if name == "wides":
                near_wide = pass_on(after(norm_near, found[condition]), near_bits)
                cross_wide = pass_on(after(norm_cross, found[condition]), cross_bits)
                wides.update({"q": near_wide, "k": near_wide, "v": cross_wide})
                found[name] = near_wide
            elif name == "olds":
                wides["o"] = pass_on(after(grad_wide, found[condition]), cross_bits)
                wides["tap"] = pass_on(after(packs, found[condition]), near_bits)
                found[name] = wides["o"]
            elif name == "resid_far":
                found[name] = send_wide(after(found["resid"], found[condition]), near_bits)
            elif name in ("q_pass", "k_pass", "v_pass", "o_pass", "tap_pass", "point_pass"):
                which = name[:-5]
                if which == "point":
                    got = after(found["resid_far"], found[condition])
                    found[name] = pass_on(got, near_bits)
                    continue
                far = after(found[which + "_far"], found[condition])
                mine = found["conv"] if which == "tap" else deltas[place[which]]
                near_copy = found["conv_near"] if which == "tap" else delta_near
                found[name] = gathered(mine, near_copy, far, peers[which])
            elif name == "tap_far":
                found[name] = send_far(after(found["conv"], found[condition]), near_bits)
            else:
                which = name[:-4]
                mine = after(deltas[place[which]], found[condition])
                found[name] = send_far(mine, peers[which])

    found["start"] = grad_parts
    found["near"] = delta_near
    previous = "start"
    open_gates()
    for step in ORDER:
        which, _, kind = step.partition("_")
        if step == "mm":
            found[step] = dot_nn(wanted(attended, previous), out_weight).astype(BF)
        elif step == "back":
            moved = wanted(grad_moved, previous)
            conv, resid = back_block(
                near, residual, grad_y, grad_parts, moved, pre, point_weight, ring_rows, group
            )
            names = [name for name in NEEDED if name in found]
            conv, resid, gots = lax.optimization_barrier(
                (conv, resid, [found[name] for name in names])
            )
            found.update(dict(zip(names, gots)))
            found["conv"], found["resid"], found[step] = conv, resid, conv
            found["conv_near"] = to_peer(conv, bits[0]) if bits else None
        elif kind == "sum":
            if which == "tap":
                narrow = wanted(found["tap_pass"], previous)
                total = tap_sum(offset, wides["tap"], narrow, halves, ring_rows)
            elif which == "point":
                total = point_sum(wides["tap"], wanted(found["point_pass"], previous), halves)
            else:
                narrow = wanted(found[which + "_pass"], previous)
                total = weight_sum(wides[which], narrow, place[which], halves)
            found[step] = total
            found[which + "_got"] = send_half(total, rest[which])
        elif kind == "add":
            got = wanted(found[which + "_got"], previous)
            found[step] = add_half(found[which + "_sum"], got, rest[which])
        elif kind == "end":
            kept, got = wanted(found[which + "_add"], previous)
            found[step] = last_block(kept, got, "taps" if which == "tap" else "plain")
        if kind == "add":
            found[step + "_kept"] = found[step][0]
            previous = step + "_kept"
        else:
            previous = step
        open_gates()

    attn_part = after(found["mm"], found["back"])
    if pair:
        attn_rows = attn_part[:rows].astype(F32) + swap_seq(attn_part[rows:]).astype(F32)
        res_own = residual[:rows]
    else:
        attn_rows = lax.psum_scatter(attn_part, "seq", scatter_dimension=0, tiled=True)
        attn_rows = attn_rows.astype(F32)
        res_own = lax.dynamic_slice_in_dim(residual, me_seq * rows, rows, 0)
    output = (res_own.astype(F32) + attn_rows).astype(BF)[None]
    return (
        output,
        found["tap_end"],
        found["point_end"].T,
        found["q_end"],
        found["k_end"],
        found["v_end"],
        found["o_end"].T,
    )


def solution(mesh):
    placed = (
        P("dp", "seq", None),
        P(None, "seq", None),
        P("seq", None),
        P("seq", None),
        P("seq", None),
        P("seq", None),
        P("seq", None),
        P("dp", "seq", None),
    )
    return jax.shard_map(
        shards,
        mesh=mesh,
        in_specs=placed,
        out_specs=(
            P("dp", "seq", None),
            P(None, "dp", "seq"),
            P("seq", "dp"),
            P("dp", "seq"),
            P("dp", "seq"),
            P("dp", "seq"),
            P("seq", "dp"),
        ),
        check_vma=False,
    )
```

```python
import functools
import math

import jax
import jax.numpy as jnp
from jax import lax
from jax.experimental import pallas as pl
from jax.experimental.pallas import tpu as pltpu
from jax.sharding import PartitionSpec as P

HSIZE = 192
DILATION_STEP = 16
EPSILON = 1e-06
SOFT_CAP = 6.0
GELU_C = math.sqrt(2.0 / math.pi)
GELU_A = 0.044715
BF = jnp.bfloat16
F32 = jnp.float32
ORDER = (
    "q_sum", "v_sum", "back", "q_add", "k_sum", "tap_sum", "mm", "v_add", "k_add", "q_end",
    "o_sum", "v_end", "point_sum", "tap_add", "o_add", "k_end", "point_add", "tap_end", "o_end",
    "point_end",
)
SENDS = (
    ("q_far", "start"), ("v_far", "start"), ("k_far", "q_far"), ("wides", "near"),
    ("q_pass", "start"), ("v_pass", "start"), ("tap_far", "back"), ("resid_far", "tap_far"),
    ("k_pass", "q_add_kept"), ("o_far", "back"), ("tap_pass", "back"), ("olds", "near"),
    ("o_pass", "tap_sum"), ("point_pass", "tap_sum"),
)
NEEDED = ("q_got",)
NO_COST = pl.CostEstimate(flops=0, bytes_accessed=0, transcendentals=0)


def gelu(x):
    return 0.5 * x * (1.0 + jnp.tanh(GELU_C * (x + GELU_A * (x * x * x))))


def gelu_slope(x):
    t = jnp.tanh(GELU_C * (x + GELU_A * (x * x * x)))
    return 0.5 * (1.0 + t) + 0.5 * x * (1.0 - t * t) * GELU_C * (1.0 + 3.0 * GELU_A * x * x)


def dot_nn(a, b):
    return lax.dot_general(a, b, (((1,), (0,)), ((), ())), preferred_element_type=F32)


def dot_nt(a, b):
    return lax.dot_general(a, b, (((1,), (1,)), ((), ())), preferred_element_type=F32)


def dot_tn(a, b):
    return lax.dot_general(a, b, (((0,), (0,)), ((), ())), preferred_element_type=F32)


def rms_scale(x):
    return lax.rsqrt(jnp.mean(x * x, axis=-1, keepdims=True) + EPSILON)


def row_chunk(rows):
    return 128 if rows % 128 == 0 else rows


def loop_chunks(count, body):
    if count <= 2:
        for i in range(count):
            body(i)
    else:

        def step(i, carry):
            body(i)
            return carry

        lax.fori_loop(0, count, step, 0)


def rows_at(i, size):
    if isinstance(i, int):
        return pl.ds(i * size, size)
    return pl.ds(pl.multiple_of(i * size, size), size)


def emit_rows(starts, wide, outs, rows):
    peers = len(outs) if len(outs) < 3 else 4
    parts = starts.shape[0] // peers
    size = rows // parts
    for p in range(peers):
        out, base = (outs[2], (p - 2) * rows) if p > 1 else (outs[p], 0)
        for k in range(parts):
            at = pl.multiple_of(starts[p * parts + k], 16)
            out[base + k * size : base + (k + 1) * size, :] = wide[pl.ds(at, size), :]


def wide_shapes(group, rows, length, extra=0):
    found = [shape_of(rows + extra, length)] * min(group, 2)
    return found + [shape_of(2 * rows + extra, length)] * (group > 2)


def shifted_sum(first, middle, last, offset):
    length = middle.shape[0]
    step = DILATION_STEP
    pos = lax.rem(lax.broadcasted_iota(jnp.int32, (length, 1), 0) + offset, length)
    down = jnp.concatenate([first[length - step :], first[: length - step]], axis=0)
    up = jnp.concatenate([last[step:], last[:step]], axis=0)
    return jnp.where(pos >= step, down, 0.0) + middle + jnp.where(pos < length - step, up, 0.0)


def vmem_params(arrays, copies=1):
    held = sum(math.prod(t.shape) * jnp.dtype(t.dtype).itemsize for t in arrays)
    return pltpu.CompilerParams(vmem_limit_bytes=min(56 << 20, copies * held + (8 << 20)))


def call(kernel, out_shape, operands, smem=1, scratch=()):
    specs = [pl.BlockSpec(memory_space=pltpu.SMEM)] * smem
    specs += [pl.BlockSpec(memory_space=pltpu.VMEM)] * (len(operands) - smem)
    return pl.pallas_call(
        kernel,
        out_shape=out_shape,
        in_specs=specs,
        out_specs=[pl.BlockSpec(memory_space=pltpu.VMEM)] * len(out_shape),
        scratch_shapes=list(scratch),
        compiler_params=vmem_params([*operands, *out_shape, *scratch]),
        cost_estimate=NO_COST,
    )(*operands)


def shape_of(rows, cols, dtype=BF):
    return jax.ShapeDtypeStruct((rows, cols), dtype)


def parts_shape(count, rows, cols):
    return jax.ShapeDtypeStruct((count, rows, cols), BF)


def store_parts(parts_ref, place, value):
    rows, size = parts_ref.shape[1], value.shape[0]
    for at in range(0, size, min(rows, size)):
        j, first = divmod(place * size + at, rows)
        parts_ref[j, first : first + min(rows, size), :] = value[at : at + min(rows, size)]


def summed_rows(parts_ref, moved, j, here):
    total = parts_ref[j, here, :].astype(F32)
    for ref in moved:
        total = total + ref[1 - j, here, :].astype(F32)
    return total


def piece_rows(j, rows, i, size):
    if isinstance(i, int):
        return pl.ds(j * rows + i * size, size)
    return pl.ds(pl.multiple_of(j * rows + i * size, size), size)


def scaled_rows(rows, factor, *ahead):
    def kernel(*refs):
        refs[-1][...] = (refs[0][...].astype(F32) * factor).astype(BF)

    return call(kernel, [shape_of(*rows.shape)], [rows, *ahead], 0)[0]


def conv_block(offset, pieces, taps, point):
    count = len(pieces)
    rows, channels = pieces[0].shape
    length = rows * count
    inner = point.shape[0]

    def kernel(*refs):
        offset_ref, ins = refs[0], refs[1 : 1 + count]
        taps_ref, point_ref, pre_ref, parts_ref, mid_ref, act_ref, prod = refs[1 + count :]
        size = row_chunk(rows)
        for j in range(count):

            def body(i, j=j):
                x = ins[j][rows_at(i, size), :].astype(F32)
                act_ref[piece_rows(j, rows, i, size), :] = gelu(x * rms_scale(x)).astype(BF)

            loop_chunks(rows // size, body)
        big = min(256, length)

        def product(i):
            here = rows_at(i, big)
            prod[here, :] = dot_nt(act_ref[here, :], taps_ref[...])

        loop_chunks(length // big, product)
        pre = shifted_sum(
            prod[:, :inner], prod[:, inner : 2 * inner], prod[:, 2 * inner :], offset_ref[0]
        )
        pre_ref[...] = pre
        mid_ref[...] = gelu(pre).astype(BF)
        for c in range(length // big):
            total = dot_nn(mid_ref[c * big : (c + 1) * big, :], point_ref[...])
            store_parts(parts_ref, c, total.astype(BF))

    outs = [
        shape_of(length, inner, F32),
        parts_shape(count, rows, channels),
        shape_of(length, inner),
        shape_of(length, channels),
    ]
    scratch = [pltpu.VMEM((length, 3 * inner), F32)]
    return call(kernel, outs, [offset, *pieces, taps, point], 1, scratch)


def pack_block(starts, act, middle, ring_rows, group):
    length, inner = middle.shape
    channels = act.shape[1]

    def kernel(*refs):
        starts_ref, act_ref, mid_ref = refs[:3]
        sent, wide = refs[3:-1], refs[-1]
        size = row_chunk(length)

        def body(i):
            here = rows_at(i, size)
            wide[:, here] = act_ref[here, :].T

        loop_chunks(length // size, body)
        emit_rows(starts_ref, wide, sent, ring_rows)
        turned = mid_ref[...].T
        for out in sent:
            out[out.shape[0] - inner :, :] = turned

    outs = wide_shapes(group, ring_rows, length, inner)
    scratch = [pltpu.VMEM((channels, length), BF)]
    return call(kernel, outs, [starts, act, middle], 1, scratch)


def head_grads(grad_y, out_w):
    def kernel(gy_ref, wo_ref, out_ref):
        out_ref[...] = dot_nt(gy_ref[...], wo_ref[...]).astype(BF)

    return call(kernel, [shape_of(grad_y.shape[0], out_w.shape[0])], [grad_y, out_w], 0)[0]


def norm_block(near, cross, pieces, parts, moved, ring_rows, group):
    count = len(pieces)
    rows, channels = pieces[0].shape
    length = rows * count

    def kernel(*refs):
        near_ref, cross_ref = refs[:2]
        ins = refs[2 : 2 + count]
        parts_ref = refs[2 + count]
        adds = refs[3 + count : 3 + count + len(moved)]
        rest = refs[3 + count + len(moved) :]
        res_ref, norm_ref = rest[:2]
        sent, wide = rest[2:-1], rest[-1]
        size = row_chunk(rows)
        for j in range(count):

            def body(i, j=j):
                here = piece_rows(j, rows, i, size)
                total = summed_rows(parts_ref, adds, j, rows_at(i, size))
                res = (ins[j][rows_at(i, size), :].astype(F32) + total).astype(BF)
                res_ref[here, :] = res
                res = res.astype(F32)
                a = (res * rms_scale(res)).astype(BF)
                norm_ref[here, :] = a
                wide[:, here] = a.T

            loop_chunks(rows // size, body)
        emit_rows(near_ref, wide, sent[: len(sent) // 2], ring_rows)
        emit_rows(cross_ref, wide, sent[len(sent) // 2 :], ring_rows)

    outs = [shape_of(length, channels), shape_of(length, channels)]
    sides = wide_shapes(group, ring_rows, length)
    outs += sides + sides
    scratch = [pltpu.VMEM((channels, length), BF)]
    res = call(kernel, outs, [near, cross, *pieces, parts, *moved], 2, scratch)
    return res[0], res[1], res[2 : 2 + len(sides)], res[2 + len(sides) :]


def widen_block(starts, pieces, ring_rows, group):
    count = len(pieces)
    rows, channels = pieces[0].shape
    length = rows * count

    def kernel(*refs):
        starts_ref = refs[0]
        ins = refs[1 : 1 + count]
        whole_ref = refs[1 + count]
        sent, wide = refs[2 + count : -1], refs[-1]
        size = row_chunk(rows)
        for j in range(count):

            def body(i, j=j):
                here = piece_rows(j, rows, i, size)
                a = ins[j][rows_at(i, size), :]
                whole_ref[here, :] = a
                wide[:, here] = a.T

            loop_chunks(rows // size, body)
        emit_rows(starts_ref, wide, sent, ring_rows)

    outs = [shape_of(length, channels)] + wide_shapes(group, ring_rows, length)
    scratch = [pltpu.VMEM((channels, length), BF)]
    res = call(kernel, outs, [starts, *pieces], 1, scratch)
    return res[0], res[1:]


def attention_block(normed, grad_heads, query_w, key_w, value_w, count):
    length, channels = normed.shape
    rows = length // count
    features = query_w.shape[0]
    heads = features // HSIZE
    joined = 2 if heads % 2 == 0 else 1
    inv_root = 1.0 / math.sqrt(HSIZE)
    chunk = min(256, length)

    def one_head(q, k, v, g):
        dq, at = [], []
        dk = dv = None
        for c in range(length // chunk):
            qc = q[c * chunk : (c + 1) * chunk]
            gc = g[c * chunk : (c + 1) * chunk]
            ratio = jnp.tanh(dot_nt(qc, k) * (inv_root / SOFT_CAP))
            unnormed = jnp.exp(SOFT_CAP * ratio)
            soft = unnormed / jnp.sum(unnormed, axis=-1, keepdims=True)
            low = soft.astype(BF)
            at.append(dot_nn(low, v))
            gs = dot_nt(gc, v)
            gs = soft * (gs - jnp.sum(soft * gs, axis=-1, keepdims=True))
            gs = (gs * (1.0 - ratio * ratio)).astype(BF)
            dq.append(dot_nn(gs, k) * inv_root)
            dk_c = dot_tn(gs, qc)
            dv_c = dot_tn(low, gc)
            dk = dk_c if dk is None else dk + dk_c
            dv = dv_c if dv is None else dv + dv_c
        return side(dq, 0), dk * inv_root, dv, side(at, 0)

    def side(parts, axis):
        return parts[0] if len(parts) == 1 else jnp.concatenate(parts, axis=axis)

    def kernel(n_ref, gh_ref, wq, wk, wv, *rest):
        refs, all_ref, dn_ref = rest[:4], rest[4], rest[5]
        q_ref, k_ref, v_ref = rest[6:]

        def project(i):
            here = rows_at(i, chunk)
            n = n_ref[here, :]
            for w, ref in ((wq, q_ref), (wk, k_ref), (wv, v_ref)):
                ref[here, :] = dot_nt(n, w[...]).astype(BF)

        loop_chunks(length // chunk, project)
        for h in range(0, heads, joined):
            found = []
            for m in range(h, h + joined):
                cols = slice(m * HSIZE, (m + 1) * HSIZE)
                found.append(
                    one_head(q_ref[:, cols], k_ref[:, cols], v_ref[:, cols], gh_ref[:, cols])
                )
            cols = slice(h * HSIZE, (h + joined) * HSIZE)
            for place, ref in enumerate(refs):
                value = side([t[place] for t in found], 1).astype(BF)
                ref[:, cols] = value
                all_ref[place, :, cols] = value
        for c in range(length // chunk):
            here = pl.ds(c * chunk, chunk)
            total = None
            for ref, w in zip(refs, (wq, wk, wv)):
                term = dot_nn(ref[here, :], w[...])
                total = term if total is None else total + term
            store_parts(dn_ref, c, total.astype(BF))

    outs = [shape_of(length, features)] * 4
    outs += [parts_shape(4, length, features), parts_shape(count, rows, channels)]
    scratch = [pltpu.VMEM((length, features), BF)] * 3
    return call(kernel, outs, [normed, grad_heads, query_w, key_w, value_w], 0, scratch)


def back_block(starts, residual, grad_y, parts, moved, pre, point, ring_rows, group):
    length, channels = residual.shape
    inner = point.shape[0]
    count, rows = parts.shape[:2]

    def kernel(*refs):
        starts_ref, res_ref, gy_ref, parts_ref = refs[:4]
        adds = refs[4 : 4 + len(moved)]
        pre_ref, point_ref = refs[4 + len(moved) : 6 + len(moved)]
        rest = refs[6 + len(moved) :]
        gc_ref = rest[0]
        sent = rest[1:-2]
        wide, resid_grad = rest[-2:]
        size = row_chunk(rows)
        for j in range(count):

            def body(i, j=j):
                here = piece_rows(j, rows, i, size)
                gn = summed_rows(parts_ref, adds, j, rows_at(i, size))
                res = res_ref[here, :].astype(F32)
                scale = rms_scale(res)
                inner_mean = jnp.mean(gn * res, axis=-1, keepdims=True)
                a = gy_ref[here, :].astype(F32) + (
                    scale * gn - res * (scale * scale * scale) * inner_mean
                )
                a = a.astype(BF)
                resid_grad[here, :] = a
                wide[:, here] = a.T

            loop_chunks(rows // size, body)
        big = min(256, length)

        def product(i):
            here = rows_at(i, big)
            gm = dot_nt(resid_grad[here, :], point_ref[...])
            gc_ref[here, :] = (gelu_slope(pre_ref[here, :]) * gm).astype(BF)

        loop_chunks(length // big, product)
        emit_rows(starts_ref, wide, sent, ring_rows)

    outs = [shape_of(length, inner)] + wide_shapes(group, ring_rows, length)
    scratch = [pltpu.VMEM((channels, length), BF), pltpu.VMEM((length, channels), BF)]
    res = call(
        kernel,
        outs,
        [starts, residual, grad_y, parts, *moved, pre, point],
        1,
        scratch,
    )
    return res[0], res[1:]


def store_halves(outs, total, side, cols):
    half = total.shape[0] // len(outs)
    for k, out in enumerate(outs):
        part = total[k * half : (k + 1) * half]
        out[:, side * cols : (side + 1) * cols] = part


def wide_rows(ref, place, rows):
    return ref[rows : 2 * rows, :] if place == 3 else ref[:rows, :]


def weight_sum(wides, narrows, place, halves):
    group = len(wides)
    rows = wides[0].shape[0]
    cols = narrows[0].shape[1]

    def kernel(*refs):
        total = None
        for p in range(group):
            b_ref = refs[group + p]
            b = b_ref[place] if len(b_ref.shape) == 3 else b_ref[...]
            term = dot_nn(wide_rows(refs[p], p, rows), b)
            total = term if total is None else total + term
        store_halves(refs[2 * group :], total.astype(BF), 0, cols)

    return call(kernel, [shape_of(rows // halves, cols)] * halves, [*wides, *narrows], 0)


def tap_sum(offset, packs, conv_narrows, halves, rows):
    group = len(packs)
    length, inner = conv_narrows[0].shape
    step = DILATION_STEP

    def kernel(offset_ref, *refs):
        pack_refs, conv_refs = refs[:group], refs[group : 2 * group]
        outs = refs[2 * group :]
        pos = lax.rem(lax.broadcasted_iota(jnp.int32, (length, 1), 0) + offset_ref[0], length)
        total = [None] * 3
        for p in range(group):
            a = wide_rows(pack_refs[p], p, rows)
            b = conv_refs[p][...]
            up = jnp.concatenate([b[step:], b[:step]], axis=0).astype(F32)
            down = jnp.concatenate([b[length - step :], b[: length - step]], axis=0).astype(F32)
            first = jnp.where(pos < length - step, up, 0.0).astype(BF)
            last = jnp.where(pos >= step, down, 0.0).astype(BF)
            terms = [dot_nn(a, moved) for moved in (first, b, last)]
            total = [t if old is None else old + t for old, t in zip(total, terms)]
        for side in range(3):
            store_halves(outs, total[side].astype(BF), side, inner)

    outs = [shape_of(rows // halves, 3 * inner)] * halves
    return call(kernel, outs, [offset, *packs, *conv_narrows], 1)


def point_sum(packs, resid_wides, halves):
    group = len(packs)
    rows = resid_wides[0].shape[0]
    inner = packs[0].shape[0] - rows

    def kernel(*refs):
        pack_refs, wide_refs = refs[:group], refs[group : 2 * group]
        total = None
        for p in range(group):
            middle = pack_refs[p][pack_refs[p].shape[0] - inner :, :]
            term = dot_nt(wide_rows(wide_refs[p], p, rows), middle)
            total = term if total is None else total + term
        store_halves(refs[2 * group :], total.astype(BF), 0, inner)

    outs = [shape_of(rows // halves, inner)] * halves
    return call(kernel, outs, [*packs, *resid_wides], 0)


def add_block(kept, got):
    rows, cols = kept.shape
    half = rows // 2

    def kernel(kept_ref, got_ref, first_ref, second_ref):
        first_ref[...] = kept_ref[:half, :].astype(F32) + got_ref[:half, :].astype(F32)
        second = kept_ref[half:, :].astype(F32) + got_ref[half:, :].astype(F32)
        second_ref[...] = second.astype(BF)

    return call(kernel, [shape_of(half, cols, F32), shape_of(half, cols)], [kept, got], 0)


def last_block(kept, got, form):
    rows, cols = kept.shape
    if form == "taps":
        out = jax.ShapeDtypeStruct((3, rows, cols // 3), F32)
    else:
        out = shape_of(rows, cols, F32)

    def kernel(*refs):
        total = refs[0][...].astype(F32)
        for ref in refs[1:-1]:
            total = total + ref[...].astype(F32)
        out_ref = refs[-1]
        if form == "taps":
            for k in range(3):
                out_ref[k] = total[:, k * (cols // 3) : (k + 1) * (cols // 3)]
        else:
            out_ref[...] = total

    return call(kernel, [out], [kept] if got is None else [kept, got], 0)[0]


def after(value, *others):
    return lax.optimization_barrier((value, others))[0]


def shards(
    inputs,
    dilated_tap_weight,
    point_weight,
    query_weight,
    key_weight,
    value_weight,
    out_weight,
    cotangent,
):
    channels = inputs.shape[2]
    own = inputs[0]
    rows = own.shape[0]
    n_seq = lax.axis_size("seq")
    n_dp = lax.axis_size("dp")
    length = rows * n_seq
    pair = n_seq == 2
    block = channels // n_dp
    inner = point_weight.shape[0]
    features = query_weight.shape[0]
    inv_tokens = 1.0 / math.sqrt(inputs.shape[0] * n_dp * length)

    bits = [1 << i for i in range(n_dp.bit_length() - 1)]
    near_bits, near_rest = bits[:2], bits[2:]
    cross_bits, cross_rest = near_bits, near_rest
    if len(bits) > 2:
        cross_bits, cross_rest = [bits[0], bits[2]], [bits[1], *bits[3:]]
    group = 1 << len(near_bits)
    ring_rows = channels // group
    halves = 2 if near_rest else 1

    me_dp = lax.axis_index("dp")
    me_seq = lax.axis_index("seq")

    def combos(of):
        found = [0]
        for bit in of:
            found += [value | bit for value in found]
        return found

    def starts_of(peers, rest):
        order = combos(rest[::-1])
        places = [peer ^ k for peer in combos(peers) for k in order]
        return ((me_dp ^ jnp.array(places, jnp.int32)) * block).astype(jnp.int32)

    near = starts_of(near_bits, near_rest)
    cross = starts_of(cross_bits, cross_rest)
    offset = (me_seq * rows if pair else jnp.int32(0)).astype(jnp.int32).reshape(1)

    def swap_seq(x):
        return lax.ppermute(x, "seq", [(0, 1), (1, 0)])

    def to_peer(x, bit):
        if bit == 0:
            return x
        return lax.ppermute(x, "dp", [(i, i ^ bit) for i in range(n_dp)])

    def gather_seq(x):
        if pair:
            return [x, swap_seq(x)]
        return [lax.all_gather(x, "seq", axis=0, tiled=True)]

    def add_seq(parts):
        if pair:
            return parts, [swap_seq(parts)]
        summed = lax.psum_scatter(parts[0], "seq", scatter_dimension=0, tiled=True)
        return lax.all_gather(summed, "seq", axis=0, tiled=True)[None], []

    def send_wide(pieces, peers):
        return [pieces[0]] + [to_peer(piece, p) for piece, p in zip(pieces[1:], peers)]

    def pass_on(got, peers):
        return list(got) + ([to_peer(got[2], peers[0])] if len(peers) > 1 else [])

    def send_far(x, peers):
        return to_peer(x, peers[1]) if len(peers) > 1 else None

    def gathered(x, near_copy, far_copy, peers):
        return pass_on([x, near_copy, far_copy][: 1 + len(peers)], peers)

    def send_half(totals, rest):
        return to_peer(totals[1], rest[0]) if rest else None

    def add_half(totals, got, rest):
        kept = totals[0]
        for bit in rest[1:]:
            kept, sent = add_block(kept, got)
            got = to_peer(sent, bit)
        return kept, got

    pieces = gather_seq(own)
    taps = dilated_tap_weight.reshape(3 * inner, channels)
    grad_own = scaled_rows(cotangent[0], inv_tokens, own, taps, point_weight)
    grad_pieces = gather_seq(grad_own)
    pre, parts, middle, act = conv_block(offset, pieces, taps, point_weight)
    pre, parts, middle, act, grad_pieces = lax.optimization_barrier(
        (pre, parts, middle, act, grad_pieces)
    )
    parts, moved = add_seq(parts)
    packs = pack_block(near, act, middle, ring_rows, group)
    packs = send_wide(packs, near_bits)
    grad_y, grad_wide = widen_block(cross, grad_pieces, ring_rows, group)
    grad_wide = send_wide(grad_wide, cross_bits)
    grad_heads = head_grads(grad_y, out_weight)
    moved = after(moved, packs, grad_wide, grad_heads)
    residual, normed, norm_near, norm_cross = norm_block(
        near, cross, pieces, parts, moved, ring_rows, group
    )
    norm_near = send_wide(norm_near, near_bits)
    norm_cross = send_wide(norm_cross, cross_bits)

    *deltas, delta_all, grad_parts = attention_block(
        normed, grad_heads, query_weight, key_weight, value_weight, len(pieces)
    )
    grad_parts, deltas, delta_all, norm_near, norm_cross = lax.optimization_barrier(
        (grad_parts, deltas, delta_all, norm_near, norm_cross)
    )
    attended = deltas[3]
    grad_parts, grad_moved = add_seq(grad_parts)
    delta_near = to_peer(delta_all, bits[0]) if bits else None

    peers = {name: near_bits for name in ("q", "k", "tap", "point")}
    peers.update({name: cross_bits for name in ("v", "o")})
    rest = {name: cross_rest if peers[name] is cross_bits else near_rest for name in peers}
    place = {"q": 0, "k": 1, "v": 2, "o": 3}
    found = {}

    def wanted(value, *names):
        names = [name for name in names if name in found]
        return after(value, *[found[name] for name in names]) if names else value

    wides = {"q": norm_near, "k": norm_near, "v": norm_cross, "o": grad_wide, "tap": packs}

    def open_gates():
        for name, condition in SENDS:
            if name in found or condition not in found:
                continue
            if name == "wides":
                near_wide = pass_on(after(norm_near, found[condition]), near_bits)
                cross_wide = pass_on(after(norm_cross, found[condition]), cross_bits)
                wides.update({"q": near_wide, "k": near_wide, "v": cross_wide})
                found[name] = near_wide
            elif name == "olds":
                wides["o"] = pass_on(after(grad_wide, found[condition]), cross_bits)
                wides["tap"] = pass_on(after(packs, found[condition]), near_bits)
                found[name] = wides["o"]
            elif name == "resid_far":
                found[name] = send_wide(after(found["resid"], found[condition]), near_bits)
            elif name in ("q_pass", "k_pass", "v_pass", "o_pass", "tap_pass", "point_pass"):
                which = name[:-5]
                if which == "point":
                    got = after(found["resid_far"], found[condition])
                    found[name] = pass_on(got, near_bits)
                    continue
                far = after(found[which + "_far"], found[condition])
                mine = found["conv"] if which == "tap" else deltas[place[which]]
                near_copy = found["conv_near"] if which == "tap" else delta_near
                found[name] = gathered(mine, near_copy, far, peers[which])
            elif name == "tap_far":
                found[name] = send_far(after(found["conv"], found[condition]), near_bits)
            else:
                which = name[:-4]
                mine = after(deltas[place[which]], found[condition])
                found[name] = send_far(mine, peers[which])

    found["start"] = grad_parts
    found["near"] = delta_near
    previous = "start"
    open_gates()
    for step in ORDER:
        which, _, kind = step.partition("_")
        if step == "mm":
            found[step] = dot_nn(wanted(attended, previous), out_weight).astype(BF)
        elif step == "back":
            moved = wanted(grad_moved, previous)
            conv, resid = back_block(
                near, residual, grad_y, grad_parts, moved, pre, point_weight, ring_rows, group
            )
            names = [name for name in NEEDED if name in found]
            conv, resid, gots = lax.optimization_barrier(
                (conv, resid, [found[name] for name in names])
            )
            found.update(dict(zip(names, gots)))
            found["conv"], found["resid"], found[step] = conv, resid, conv
            found["conv_near"] = to_peer(conv, bits[0]) if bits else None
        elif kind == "sum":
            if which == "tap":
                narrow = wanted(found["tap_pass"], previous)
                total = tap_sum(offset, wides["tap"], narrow, halves, ring_rows)
            elif which == "point":
                total = point_sum(wides["tap"], wanted(found["point_pass"], previous), halves)
            else:
                narrow = wanted(found[which + "_pass"], previous)
                total = weight_sum(wides[which], narrow, place[which], halves)
            found[step] = total
            found[which + "_got"] = send_half(total, rest[which])
        elif kind == "add":
            got = wanted(found[which + "_got"], previous)
            found[step] = add_half(found[which + "_sum"], got, rest[which])
        elif kind == "end":
            kept, got = wanted(found[which + "_add"], previous)
            found[step] = last_block(kept, got, "taps" if which == "tap" else "plain")
        if kind == "add":
            found[step + "_kept"] = found[step][0]
            previous = step + "_kept"
        else:
            previous = step
        open_gates()

    attn_part = after(found["mm"], found["back"])
    if pair:
        attn_rows = attn_part[:rows].astype(F32) + swap_seq(attn_part[rows:]).astype(F32)
        res_own = residual[:rows]
    else:
        attn_rows = lax.psum_scatter(attn_part, "seq", scatter_dimension=0, tiled=True)
        attn_rows = attn_rows.astype(F32)
        res_own = lax.dynamic_slice_in_dim(residual, me_seq * rows, rows, 0)
    output = (res_own.astype(F32) + attn_rows).astype(BF)[None]
    return (
        output,
        found["tap_end"],
        found["point_end"].T,
        found["q_end"],
        found["k_end"],
        found["v_end"],
        found["o_end"].T,
    )


def solution(mesh):
    placed = (
        P("dp", "seq", None),
        P(None, "seq", None),
        P("seq", None),
        P("seq", None),
        P("seq", None),
        P("seq", None),
        P("seq", None),
        P("dp", "seq", None),
    )
    return jax.shard_map(
        shards,
        mesh=mesh,
        in_specs=placed,
        out_specs=(
            P("dp", "seq", None),
            P(None, "dp", "seq"),
            P("seq", "dp"),
            P("dp", "seq"),
            P("dp", "seq"),
            P("dp", "seq"),
            P("seq", "dp"),
        ),
        check_vma=False,
    )
```
